128 devices in a mesh: node: 16 (over z, y), local: 8 (over x, core).
Axes of the slice: x: 4, y: 4, z: 4, core: 2. Of those that a mesh axis runs over, the one named last changes fastest.
Arguments:
- tokens: bfloat16 [16384, 3584], P(('node', 'local')), may hold values from -6 to 6
- cotangent: bfloat16 [16384, 3584], P(('node', 'local')), may hold values from -0.75 to 0.75
- expert_ids: int32 [16384, 8], P(('node', 'local')), may hold values from 0 to 127, as said below
- gate_fixed: int32 [16384, 8], P(('node', 'local')), may hold values from 1 to 65535
- w_up: bfloat16 [128, 3584, 1024], P(('node', 'local')), may hold values from -0.09375 to 0.09375
- w_down: bfloat16 [128, 1024, 3584], P(('node', 'local')), may hold values from -0.1875 to 0.1875
Outputs:
- grad_input: bfloat16 [16384, 3584], P(('node', 'local'))
- grad_gate: bfloat16 [16384, 8], P(('node', 'local'))
The draws below stay inside these ranges and needn't reach their ends.
Inputs may be any that keep to these rules, and one draw needn't show every extreme that they name: `expert_ids`: expert e belongs to node group e // 8 (the group of devices with one index of node). Each row names 8 different experts, exactly two in each of 4 different node groups. In the 128 rows of one device every node group is named by exactly 32 rows, and no expert is named by more than 10 rows.
All inputs are finite; a program needn't handle non-finite values.
Results may differ from the reference program's by a relative error of at most 0.013.
Values may be sent and summed in bfloat16 or wider, within the bound.
No kernel may reach another device: no remote copies, remote signals or barrier semaphores. Data moves between devices by JAX's collectives and lax.ppermute only.
A program may use at most 192 MiB of HBM per device.

```python
import jax
import jax.numpy as jnp
from jax import lax

D = 3584
HID = 1024
TOP = 8
NODES_MAX = 4
TOK_DEV = 128
EXPERTS = 128
TOKENS = 16384
CAP = 10
N_NODE = 16
N_LOCAL = 8


def draw_expert_ids(key, part):
    key = jax.random.fold_in(key, 7)
    keys = jax.random.split(key, 5)
    blocks = N_NODE * N_LOCAL
    middle = N_LOCAL // 2
    period = 4 * N_LOCAL + 1
    hot_local = jax.random.randint(keys[0], (N_NODE,), 0, N_LOCAL)
    local_range = jnp.arange(N_LOCAL, dtype=jnp.int32)
    scores = jax.random.randint(keys[1], (blocks, N_NODE, N_LOCAL), 0, 1 << 20) * N_LOCAL + local_range[None, None, :]
    is_hot = local_range[None, :] == hot_local[:, None]
    scores = jnp.where(is_hot[None, :, :], -1, scores)
    listed = jnp.argsort(scores, axis=-1, stable=True).astype(jnp.int32)
    sequence = jnp.concatenate([listed[..., :middle], listed[..., :1], listed[..., middle:], listed, listed, listed], axis=-1)
    node_scores = jax.random.randint(keys[2], (blocks, N_NODE), 0, 1 << 20) * N_NODE + jnp.arange(N_NODE, dtype=jnp.int32)[None, :]
    node_order = jnp.argsort(node_scores, axis=-1, stable=True).astype(jnp.int32)
    row_scores = jax.random.randint(keys[3], (blocks, TOK_DEV), 0, 1 << 20) * TOK_DEV + jnp.arange(TOK_DEV, dtype=jnp.int32)[None, :]
    pattern = jnp.argsort(row_scores, axis=-1, stable=True).astype(jnp.int32)
    counter = 4 * pattern[:, :, None] + jnp.arange(NODES_MAX, dtype=jnp.int32)[None, None, :]
    node_pos = counter % N_NODE
    ordinal = counter // N_NODE
    node = jnp.take_along_axis(node_order, node_pos.reshape(blocks, -1), axis=1).reshape(blocks, TOK_DEV, NODES_MAX)
    block_index = jnp.arange(blocks, dtype=jnp.int32)[:, None, None]
    seq_rows = sequence[block_index, node]
    seq_pos = (2 * ordinal[..., None] + jnp.arange(2, dtype=jnp.int32)[None, None, None, :]) % period
    local = jnp.take_along_axis(seq_rows, seq_pos, axis=-1)
    experts = (node[..., None] * N_LOCAL + local).reshape(blocks, TOK_DEV, TOP)
    slot_scores = jax.random.randint(keys[4], (blocks, TOK_DEV, TOP), 0, 1 << 20) * TOP + jnp.arange(TOP, dtype=jnp.int32)[None, None, :]
    order = jnp.argsort(slot_scores, axis=-1, stable=True).astype(jnp.int32)
    experts = jnp.take_along_axis(experts, order, axis=-1)
    return experts.reshape(TOKENS, TOP).astype(jnp.int32)


def with_ends(drawn, stream_key, low, largest):
    dims = drawn.shape
    index_at = [jax.random.randint(jax.random.fold_in(stream_key, axis), (), 0, dims[axis]) for axis in range(len(dims))]
    drawn = drawn.at[tuple(index_at)].set(low)
    longest = dims.index(max(dims))
    index_at[longest] = (index_at[longest] + 1) % dims[longest]
    return drawn.at[tuple(index_at)].set(largest)


def block_levels(rng, shape, cuts, least, top_value):
    factor_of = 1.0
    for axis_at, parts in cuts:
        heights = jax.random.uniform(jax.random.fold_in(jax.random.fold_in(rng, 6), axis_at), (parts,), jnp.float32, least / len(cuts), top_value / len(cuts))
        factor_of = factor_of * jnp.repeat(jnp.exp(heights), shape[axis_at] // parts).reshape((-1,) + (1,) * (len(shape) - 1 - axis_at))
    return factor_of


def gaussian(own_key, shape, deviation, bound, shards=(), held_as=jnp.bfloat16):
    entries = jax.random.normal(own_key, shape, jnp.float32) * deviation
    if len(shards) > 0:
        entries = block_levels(own_key, shape, shards, -0.22, 0.18) * entries
    return jnp.clip(entries, min=-bound, max=bound).astype(held_as)


def setup_inputs(seed: int = 0) -> dict:
    splits = jax.random.split(jax.random.key(seed), 7)
    return {
        "tokens": gaussian(splits[0], (TOKENS, D), 1.0, 6.0, ((0, 128),)),
        "cotangent": gaussian(splits[1], (TOKENS, D), 0.125, 0.75, ((0, 128),)),
        "expert_ids": draw_expert_ids(jax.random.fold_in(splits[6], 71), 0),
        "gate_fixed": with_ends(jax.random.randint(splits[3], (TOKENS, TOP), 1, 65536), jax.random.fold_in(splits[3], 1), 1, 65535).astype(jnp.int32),
        "w_up": gaussian(splits[4], (EXPERTS, D, HID), D ** -0.5, 0.09375, ((0, 128),)),
        "w_down": gaussian(splits[5], (EXPERTS, HID, D), HID ** -0.5, 0.1875, ((0, 128),)),
    }


def slot_positions(expert_ids):
    hits = jnp.sum((expert_ids[:, :, None] == jnp.arange(EXPERTS, dtype=jnp.int32)[None, None, :]).astype(jnp.int32), axis=1)
    blocks = hits.reshape(N_NODE * N_LOCAL, TOK_DEV, EXPERTS)
    before = (jnp.cumsum(blocks, axis=1) - blocks).reshape(TOKENS, EXPERTS)
    return jnp.take_along_axis(before, expert_ids, axis=1).astype(jnp.int32)


def reference(tokens, cotangent, expert_ids, gate_fixed, w_up, w_down):
    rows_per = N_NODE * N_LOCAL * CAP
    position = slot_positions(expert_ids)
    token_index = jnp.arange(TOKENS, dtype=jnp.int32)
    source = token_index // TOK_DEV
    column = source[:, None] * CAP + position
    flat = (expert_ids * rows_per + column).reshape(-1)
    owner = jnp.full((EXPERTS * rows_per,), TOKENS, jnp.int32).at[flat].set(jnp.repeat(token_index, TOP))
    slot_of = jnp.zeros((EXPERTS * rows_per,), jnp.int32).at[flat].set(jnp.tile(jnp.arange(TOP, dtype=jnp.int32), TOKENS))
    owner = owner.reshape(EXPERTS, rows_per)
    slot_of = slot_of.reshape(EXPERTS, rows_per)
    padded_x = jnp.concatenate([tokens, jnp.zeros((1, D), tokens.dtype)], axis=0)
    padded_dy = jnp.concatenate([cotangent, jnp.zeros((1, D), cotangent.dtype)], axis=0)
    gate = jnp.concatenate([gate_fixed.astype(jnp.float32) / 65536.0, jnp.zeros((1, TOP), jnp.float32)], axis=0)

    def expert_step(carry, items):
        grad_acc, gate_acc = carry
        index, slot, up_w, down_w = items
        rows_x = padded_x[index]
        rows_dy = padded_dy[index]
        pre = jnp.dot(rows_x, up_w, preferred_element_type=jnp.float32)
        act = jax.nn.silu(pre).astype(jnp.bfloat16)
        back = jnp.dot(rows_dy, down_w.T, preferred_element_type=jnp.float32)
        gate_grad = jnp.sum(act.astype(jnp.float32) * back, axis=-1).astype(jnp.bfloat16)
        sig = jax.nn.sigmoid(pre)
        inner = (back * sig * (1.0 + pre * (1.0 - sig))).astype(jnp.bfloat16)
        piece = jnp.dot(inner, up_w.T, preferred_element_type=jnp.float32).astype(jnp.bfloat16)
        weight = gate[index, slot]
        grad_acc = grad_acc.at[index].add(weight[:, None] * piece.astype(jnp.float32))
        gate_acc = gate_acc.at[index, slot].set(gate_grad)
        return (grad_acc, gate_acc), None

    start = (jnp.zeros((TOKENS + 1, D), jnp.float32), jnp.zeros((TOKENS + 1, TOP), jnp.bfloat16))
    (grad_acc, gate_acc), unused = lax.scan(expert_step, start, (owner, slot_of, w_up, w_down))
    return grad_acc[:TOKENS].astype(jnp.bfloat16), gate_acc[:TOKENS]
```

```python
import jax
import jax.numpy as jnp
from jax import lax
from jax.experimental import pallas as pl
from jax.experimental.pallas import tpu as pltpu
from jax.sharding import PartitionSpec as P

CAP = 10
MAIN = 8
QUARTERS = 4
GROUP = 32
EXTRA = 128
VMEM = 56 * 1024 * 1024
BF16 = jnp.bfloat16
F32 = jnp.float32


def iota(shape, dim):
    return lax.broadcasted_iota(jnp.int32, shape, dim)


def dot(a, b):
    return jnp.dot(a, b, preferred_element_type=F32)


def dot_nt(a, b):
    return lax.dot_general(a, b, (((1,), (1,)), ((), ())), preferred_element_type=F32)


def dot_tn(a, b):
    return lax.dot_general(a, b, (((0,), (0,)), ((), ())), preferred_element_type=F32)


def slots_of(ids, first):
    tok = ids.shape[1]
    expert = first + iota((GROUP, tok), 0)
    hit = jnp.zeros((GROUP, tok), F32)
    for slot in range(ids.shape[0]):
        hit = hit + (expert == ids[slot : slot + 1, :]).astype(F32)
    earlier = (iota((tok, tok), 0) < iota((tok, tok), 1)).astype(BF16)
    before = dot(hit.astype(BF16), earlier)
    place = jnp.where(hit > 0.5, before, -1.0)
    rows = GROUP * MAIN
    spread = (iota((rows, GROUP), 0) // MAIN == iota((rows, GROUP), 1)).astype(BF16)
    return dot(spread, place.astype(BF16)), spread, expert


def picks(ids, first):
    place, spread, expert = slots_of(ids, first)
    row = iota(place.shape, 0)
    main = place == (row % MAIN).astype(F32)
    tail = place == (MAIN + row % 2).astype(F32)
    quarter = (row % MAIN) // 2
    return main, tail, quarter, spread, expert


def send_kernel(ids_ref, x_ref, out_ref):
    width = x_ref.shape[1]
    fold = width // QUARTERS
    main, tail, quarter, _, _ = picks(ids_ref[...], pl.program_id(0) * GROUP)
    out_ref[:, :width] = dot(main.astype(BF16), x_ref[...]).astype(BF16)
    total = None
    for q in range(QUARTERS):
        pick = jnp.logical_and(tail, quarter == q).astype(BF16)
        part = dot(pick, x_ref[:, q * fold : (q + 1) * fold])
        total = part if total is None else total + part
    out_ref[:, width:] = total.astype(BF16)


def send(ids_t, x):
    tok, width = x.shape
    experts = lax.axis_size("node") * lax.axis_size("local")
    wide = width + width // QUARTERS
    rows = GROUP * MAIN
    return pl.pallas_call(
        send_kernel,
        grid=(experts // GROUP,),
        in_specs=[
            pl.BlockSpec(ids_t.shape, lambda i: (0, 0)),
            pl.BlockSpec((tok, width), lambda i: (0, 0)),
        ],
        out_specs=pl.BlockSpec((rows, wide), lambda i: (i, 0)),
        out_shape=jax.ShapeDtypeStruct((experts * MAIN, wide), BF16),
        compiler_params=pltpu.CompilerParams(vmem_limit_bytes=VMEM),
        cost_estimate=pl.CostEstimate(
            flops=4 * experts * MAIN * 256 * width, bytes_accessed=2 * experts * MAIN * wide, transcendentals=0
        ),
        name="pick_rows",
    )(ids_t, x)


def unfold(rows_ref, tail_ref, width):
    fold = width // QUARTERS
    size = GROUP * MAIN
    tails = 2 * GROUP
    to = iota((size, size), 0)
    source = ((to % tails) // 2) * MAIN + (to // tails) * 2 + to % 2
    order = (source == iota((size, size), 1)).astype(BF16)
    for b in range(rows_ref.shape[0] // size):
        stack = dot(order, rows_ref[b * size : (b + 1) * size, width : width + fold]).astype(BF16)
        for q in range(QUARTERS):
            tail_ref[b * tails : (b + 1) * tails, q * fold : (q + 1) * fold] = stack[q * tails : (q + 1) * tails, :]


def pre_kernel(rows_ref, w_ref, out_ref, tail_ref):
    width = w_ref.shape[0]
    main = rows_ref.shape[0]

    @pl.when(pl.program_id(0) == 0)
    def _():
        unfold(rows_ref, tail_ref, width)

    out_ref[:main, :] = dot(rows_ref[:, :width], w_ref[...])
    out_ref[main:, :] = dot(tail_ref[...], w_ref[...])


def pre_of(rows, w_up, tile=256):
    main, wide = rows.shape
    width, hid = w_up.shape
    tails = main // QUARTERS
    return pl.pallas_call(
        pre_kernel,
        grid=(hid // tile,),
        in_specs=[
            pl.BlockSpec((main, wide), lambda i: (0, 0), pipeline_mode=pl.Buffered(1)),
            pl.BlockSpec((width, tile), lambda i: (0, i)),
        ],
        out_specs=pl.BlockSpec((main + tails, tile), lambda i: (0, i)),
        out_shape=jax.ShapeDtypeStruct((main + tails, hid), F32),
        scratch_shapes=[pltpu.VMEM((tails, width), BF16)],
        compiler_params=pltpu.CompilerParams(vmem_limit_bytes=VMEM),
        cost_estimate=pl.CostEstimate(
            flops=2 * (main + tails) * width * hid, bytes_accessed=22_000_000, transcendentals=0
        ),
        name="pre",
    )(rows, w_up)


def back_kernel(
    rows_ref, pre_ref, down_ref, up_ref, out_ref, tail_ref, inner_ref, gate_ref, piece_ref, stack_ref, fold_ref, extra_ref, sems
):
    step = pl.program_id(0)
    width = down_ref.shape[1]
    tile = down_ref.shape[0]
    hid = inner_ref.shape[1]
    main = rows_ref.shape[0]
    fold = width // QUARTERS
    tails = 2 * GROUP
    size = GROUP * MAIN
    groups = main // size
    first = hid // tile

    @pl.when(step == 0)
    def _():
        unfold(rows_ref, tail_ref, width)

    def hidden(rows, where):
        pre = pre_ref[where, :]
        back = dot_nt(rows, down_ref[...])
        sig = 1.0 / (1.0 + jnp.exp(-pre))
        act = (pre * sig).astype(BF16).astype(F32)
        inner = (back * sig * (1.0 + pre * (1.0 - sig))).astype(BF16)
        return inner, jnp.sum(act * back, axis=-1, keepdims=True)

    for j in range(first):

        @pl.when(step == j)
        def _():
            for where, rows in ((slice(0, main), rows_ref[:, :width]), (slice(main, None), tail_ref[...])):
                inner, gate = hidden(rows, where)
                inner_ref[where, j * tile : (j + 1) * tile] = inner
                if j == 0:
                    gate_ref[where, :] = gate
                else:
                    gate_ref[where, :] = gate_ref[where, :] + gate

    def copy_of(q):
        return pltpu.make_async_copy(
            piece_ref.at[q % 2], out_ref.at[:, pl.ds(q * fold, fold)], sems.at[q % 2]
        )

    fold_copy = pltpu.make_async_copy(fold_ref, out_ref.at[:, pl.ds(width, fold)], sems.at[2])
    extra_copy = pltpu.make_async_copy(extra_ref, out_ref.at[:, pl.ds(width + fold, EXTRA)], sems.at[3])

    for q in range(QUARTERS):

        @pl.when(step == first + q)
        def _():
            if q >= 2:
                copy_of(q - 2).wait()
            piece_ref[q % 2] = dot_nt(inner_ref[:main, :], up_ref[...]).astype(BF16)
            copy_of(q).start()
            if q == 0:
                pick = (iota((size, tails), 0) // MAIN == iota((size, tails), 1) // 2).astype(BF16)
                parity = iota((size, EXTRA), 0) % 2
                low = iota((size, EXTRA), 1) < EXTRA // 2
                for b in range(groups):
                    mains = gate_ref[b * size : (b + 1) * size, :].astype(BF16).astype(F32)
                    last = gate_ref[main + b * tails : main + (b + 1) * tails, :].astype(BF16).astype(F32)
                    odd = (iota((tails, EXTRA), 0) % 2 == 1)
                    last = jnp.broadcast_to(last, (tails, EXTRA))
                    even_rows = dot(pick, jnp.where(odd, 0.0, last).astype(BF16))
                    odd_rows = dot(pick, jnp.where(odd, last, 0.0).astype(BF16))
                    tail_rows = jnp.where(parity == 1, odd_rows, even_rows)
                    extra_ref[b * size : (b + 1) * size, :] = jnp.where(
                        low, jnp.broadcast_to(mains, (size, EXTRA)), tail_rows
                    ).astype(BF16)
                extra_copy.start()
            piece = dot_nt(inner_ref[main:, :], up_ref[...]).astype(BF16)
            for b in range(groups):
                stack_ref[b * size + q * tails : b * size + (q + 1) * tails, :] = piece[b * tails : (b + 1) * tails, :]
            if q == QUARTERS - 1:
                to = iota((size, size), 0)
                source = ((to % MAIN) // 2) * tails + (to // MAIN) * 2 + to % 2
                order = (source == iota((size, size), 1)).astype(BF16)
                for b in range(groups):
                    fold_ref[b * size : (b + 1) * size, :] = dot(
                        order, stack_ref[b * size : (b + 1) * size, :]
                    ).astype(BF16)
                fold_copy.start()
                copy_of(q - 1).wait()
                copy_of(q).wait()
                extra_copy.wait()
                fold_copy.wait()


def pieces_of(rows, pre, w_down, w_up, tile=256):
    main, wide = rows.shape
    hid, width = w_down.shape
    tails = main // QUARTERS
    fold = width // QUARTERS
    first = hid // tile
    return pl.pallas_call(
        back_kernel,
        grid=(first + QUARTERS,),
        in_specs=[
            pl.BlockSpec((main, wide), lambda i: (0, 0), pipeline_mode=pl.Buffered(1)),
            pl.BlockSpec((main + tails, tile), lambda i: (0, jnp.minimum(i, first - 1))),
            pl.BlockSpec((tile, width), lambda i: (jnp.minimum(i, first - 1), 0)),
            pl.BlockSpec((fold, hid), lambda i: (jnp.maximum(i - first, 0), 0)),
        ],
        out_specs=pl.BlockSpec(memory_space=pl.ANY),
        out_shape=jax.ShapeDtypeStruct((main, wide + EXTRA), BF16),
        scratch_shapes=[
            pltpu.VMEM((tails, width), BF16),
            pltpu.VMEM((main + tails, hid), BF16),
            pltpu.VMEM((main + tails, 1), F32),
            pltpu.VMEM((2, main, fold), BF16),
            pltpu.VMEM((main, fold), BF16),
            pltpu.VMEM((main, fold), BF16),
            pltpu.VMEM((main, EXTRA), BF16),
            pltpu.SemaphoreType.DMA((4,)),
        ],
        compiler_params=pltpu.CompilerParams(vmem_limit_bytes=VMEM),
        cost_estimate=pl.CostEstimate(
            flops=4 * (main + tails) * width * hid, bytes_accessed=39_000_000, transcendentals=(main + tails) * hid
        ),
        name="back_and_pieces",
    )(rows, pre, w_down, w_up)


def combine_kernel(ids_ref, gate_ref, rows_ref, out_ref, grad_ref, acc_ref, sum_ref):
    step = pl.program_id(0)
    tok, width = out_ref.shape
    fold = width // QUARTERS
    ids = ids_ref[...]
    main, tail, quarter, spread, expert = picks(ids, step * GROUP)
    high = jnp.zeros(expert.shape, F32)
    low = jnp.zeros(expert.shape, F32)
    for slot in range(ids.shape[0]):
        same = expert == ids[slot : slot + 1, :]
        fixed = gate_ref[slot : slot + 1, :]
        high = high + jnp.where(same, (fixed // 256).astype(F32), 0.0)
        low = low + jnp.where(same, (fixed % 256).astype(F32), 0.0)
    high = dot(spread, high.astype(BF16)) * (1.0 / 256.0)
    low = dot(spread, low.astype(BF16)) * (1.0 / 65536.0)

    def weights(mask):
        return jnp.concatenate([jnp.where(mask, high, 0.0), jnp.where(mask, low, 0.0)], axis=1).astype(BF16)

    @pl.when(step == 0)
    def _():
        acc_ref[...] = jnp.zeros_like(acc_ref)
        sum_ref[...] = jnp.zeros_like(sum_ref)

    both = dot_tn(weights(main), rows_ref[:, :width])
    acc_ref[...] += both[:tok, :] + both[tok:, :]
    for q in range(QUARTERS):
        both = dot_tn(weights(jnp.logical_and(tail, quarter == q)), rows_ref[:, width : width + fold])
        acc_ref[:, q * fold : (q + 1) * fold] += both[:tok, :] + both[tok:, :]

    extra = rows_ref[:, width + fold :].astype(F32)
    value = jnp.where(main, extra[:, 0:1], 0.0) + jnp.where(
        jnp.logical_and(tail, quarter == 0), extra[:, EXTRA // 2 : EXTRA // 2 + 1], 0.0
    )
    value = dot_tn(spread, value.astype(BF16))
    for slot in range(ids.shape[0]):
        part = jnp.sum(jnp.where(expert == ids[slot : slot + 1, :], value, 0.0), axis=0, keepdims=True)
        sum_ref[slot : slot + 1, :] = sum_ref[slot : slot + 1, :] + part

    @pl.when(step == pl.num_programs(0) - 1)
    def _():
        out_ref[...] = acc_ref[...].astype(BF16)
        grad_ref[...] = sum_ref[...]


def combine(ids_t, gate_t, rows, width):
    top, tok = ids_t.shape
    main, wide = rows.shape
    size = GROUP * MAIN
    return pl.pallas_call(
        combine_kernel,
        grid=(main // size,),
        in_specs=[
            pl.BlockSpec((top, tok), lambda i: (0, 0)),
            pl.BlockSpec((top, tok), lambda i: (0, 0)),
            pl.BlockSpec((size, wide), lambda i: (i, 0)),
        ],
        out_specs=[
            pl.BlockSpec((tok, width), lambda i: (0, 0)),
            pl.BlockSpec((top, tok), lambda i: (0, 0)),
        ],
        out_shape=[
            jax.ShapeDtypeStruct((tok, width), BF16),
            jax.ShapeDtypeStruct((top, tok), F32),
        ],
        scratch_shapes=[pltpu.VMEM((tok, width), F32), pltpu.VMEM((top, tok), F32)],
        compiler_params=pltpu.CompilerParams(vmem_limit_bytes=VMEM),
        name="combine",
    )(ids_t, gate_t, rows)


def exchange(rows):
    experts = lax.axis_size("node") * lax.axis_size("local")
    wide = rows.shape[1]
    blocks = rows.reshape(experts, MAIN, wide)
    blocks = lax.all_to_all(blocks, ("node", "local"), split_axis=0, concat_axis=0, tiled=True)
    return blocks.reshape(experts * MAIN, wide)


def per_device(tokens, cotangent, expert_ids, gate_fixed, w_up, w_down):
    width = tokens.shape[1]
    ids_t = expert_ids.T
    gate_t = gate_fixed.T
    rows_x = exchange(send(ids_t, tokens))
    rows_dy = exchange(send(ids_t, cotangent))
    pre = pre_of(rows_x, w_up[0])
    pieces = pieces_of(rows_dy, pre, w_down[0], w_up[0])
    grad_input, grad_gate = combine(ids_t, gate_t, exchange(pieces), width)
    return grad_input, grad_gate.T.astype(BF16)


def solution(mesh):
    split = P(("node", "local"), None)
    experts = P(("node", "local"), None, None)
    return jax.shard_map(
        per_device,
        mesh=mesh,
        in_specs=(split, split, split, split, experts, experts),
        out_specs=(split, split),
        check_vma=False,
    )
```

```python
import functools

import jax
import jax.numpy as jnp
from jax import lax
from jax.experimental import pallas as pl
from jax.experimental.pallas import tpu as pltpu
from jax.sharding import PartitionSpec as P

TOP = 8
NODES_MAX = 4
CAP = 10
MAIN = 8
QUARTERS = 4
GROUP = 32
EXTRA = 128
VMEM = 56 * 1024 * 1024
BF16 = jnp.bfloat16
F32 = jnp.float32


def iota(shape, dim):
    return lax.broadcasted_iota(jnp.int32, shape, dim)


def dot(a, b):
    return jnp.dot(a, b, preferred_element_type=F32)


def dot_nt(a, b):
    return lax.dot_general(a, b, (((1,), (1,)), ((), ())), preferred_element_type=F32)


def dot_tn(a, b):
    return lax.dot_general(a, b, (((0,), (0,)), ((), ())), preferred_element_type=F32)


def slots_of(ids, first):
    tok = ids.shape[1]
    expert = first + iota((GROUP, tok), 0)
    hit = jnp.zeros((GROUP, tok), F32)
    for slot in range(ids.shape[0]):
        hit = hit + (expert == ids[slot : slot + 1, :]).astype(F32)
    earlier = (iota((tok, tok), 0) < iota((tok, tok), 1)).astype(BF16)
    before = dot(hit.astype(BF16), earlier)
    place = jnp.where(hit > 0.5, before, -1.0)
    rows = GROUP * MAIN
    spread = (iota((rows, GROUP), 0) // MAIN == iota((rows, GROUP), 1)).astype(BF16)
    return dot(spread, place.astype(BF16)), spread, expert


def picks(ids, first):
    place, spread, expert = slots_of(ids, first)
    row = iota(place.shape, 0)
    main = place == (row % MAIN).astype(F32)
    tail = place == (MAIN + row % 2).astype(F32)
    quarter = (row % MAIN) // 2
    return main, tail, quarter, spread, expert


def places(ids, first, count):
    tok = ids.shape[1]
    expert = first + iota((count, tok), 0)
    hit = jnp.zeros((count, tok), F32)
    for slot in range(ids.shape[0]):
        hit = hit + (expert == ids[slot : slot + 1, :]).astype(F32)
    earlier = (iota((tok, tok), 0) < iota((tok, tok), 1)).astype(BF16)
    return jnp.where(hit > 0.5, dot(hit.astype(BF16), earlier), -1.0), expert


def node_kernel(ids_ref, x_ref, out_ref, *, share, nodes, local):
    width = x_ref.shape[1]
    tok = x_ref.shape[0]
    rows = out_ref.shape[0]
    some = rows // share
    ids = ids_ref[...]
    first = pl.program_id(0) * some
    node = first + iota((some, tok), 0)
    named = jnp.zeros((some, tok), F32)
    for slot in range(ids.shape[0]):
        named = jnp.maximum(named, (node == ids[slot : slot + 1, :] // local).astype(F32))
    earlier = (iota((tok, tok), 0) < iota((tok, tok), 1)).astype(BF16)
    rank = jnp.where(named > 0.5, dot(named.astype(BF16), earlier), -1.0)
    spread = (iota((rows, some), 0) // share == iota((rows, some), 1)).astype(BF16)
    wanted = (iota((rows, tok), 0) % share).astype(F32)
    pick = (dot(spread, rank.astype(BF16)) == wanted).astype(BF16)
    out_ref[:, :width] = dot(pick, x_ref[...]).astype(BF16)
    count = some * local
    place, _ = places(ids, first * local, count)
    slots = dot_nt(pick, place.astype(BF16))
    slots = jnp.where(iota((rows, count), 0) // share == iota((rows, count), 1) // local, slots, 0.0)
    lanes = (iota((count, EXTRA), 0) % local == iota((count, EXTRA), 1)).astype(BF16)
    out_ref[:, width:] = dot(slots.astype(BF16), lanes).astype(BF16)


def node_rows(ids_t, x, nodes, local):
    top, tok = ids_t.shape
    width = x.shape[1]
    share = tok * NODES_MAX // nodes
    steps = 4
    return pl.pallas_call(
        functools.partial(node_kernel, share=share, nodes=nodes, local=local),
        grid=(steps,),
        in_specs=[
            pl.BlockSpec((top, tok), lambda i: (0, 0)),
            pl.BlockSpec((tok, width), lambda i: (0, 0)),
        ],
        out_specs=pl.BlockSpec((nodes * share // steps, width + EXTRA), lambda i: (i, 0)),
        out_shape=jax.ShapeDtypeStruct((nodes * share, width + EXTRA), BF16),
        compiler_params=pltpu.CompilerParams(vmem_limit_bytes=VMEM),
        cost_estimate=pl.CostEstimate(
            flops=2 * nodes * share * 256 * width, bytes_accessed=5_000_000, transcendentals=0
        ),
        name="node_rows",
    )(ids_t, x)


def part_kernel(me_ref, rows_ref, slots_ref, *refs, share, nodes, local):
    outs, (main_ref, tail_ref) = refs[:local], refs[local:]
    x, c = me_ref[0] // 2, me_ref[0] % 2
    half = nodes // 2
    rows = half * share
    mains = half * MAIN
    tails = 2 * nodes

    def to_of(rel):
        return ((x + rel // 2) % (local // 2)) * 2 + (c + rel) % 2

    @pl.when(pl.program_id(0) == 0)
    def _():
        col, lane = iota((local * mains, EXTRA), 0), iota((local * mains, EXTRA), 1)
        spread = (lane == to_of(col // mains)).astype(BF16)
        shape = (local * mains, rows)
        row, at = iota(shape, 0), iota(shape, 1)
        fits = at // share == (row % mains) // MAIN
        slot = (row % MAIN).astype(F32)
        for g in range(2):
            place = dot_nt(spread, slots_ref[g * rows : (g + 1) * rows, :])
            main_ref[g] = jnp.logical_and(place == slot, fits).astype(BF16)
        col, lane = iota((local * tails, EXTRA), 0), iota((local * tails, EXTRA), 1)
        spread = (lane == to_of(col // tails)).astype(BF16)
        shape = (local * tails, 2 * rows)
        row, at = iota(shape, 0), iota(shape, 1)
        place = dot_nt(spread, slots_ref[...])
        fits = at // share == (row % tails) // 2
        tail_ref[...] = jnp.logical_and(place == (MAIN + row % 2).astype(F32), fits).astype(BF16)

    for g in range(2):
        got = dot(main_ref[g], rows_ref[g * rows : (g + 1) * rows, :]).astype(BF16)
        for rel in range(local):
            outs[rel][g * mains : (g + 1) * mains, :] = got[rel * mains : (rel + 1) * mains, :]
    got = dot(tail_ref[...], rows_ref[...]).astype(BF16)
    for rel in range(local):
        outs[rel][2 * mains :, :] = got[rel * tails : (rel + 1) * tails, :]


def part_rows(me, rows, nodes, local):
    total, wide = rows.shape
    width = wide - EXTRA
    share = total // nodes
    fold = width // QUARTERS
    size = nodes * CAP
    return pl.pallas_call(
        functools.partial(part_kernel, share=share, nodes=nodes, local=local),
        grid=(QUARTERS,),
        in_specs=[
            pl.BlockSpec(memory_space=pltpu.SMEM),
            pl.BlockSpec((total, fold), lambda i: (0, i)),
            pl.BlockSpec((total, EXTRA), lambda i: (0, width // EXTRA)),
        ],
        out_specs=[pl.BlockSpec((size, fold), lambda i: (0, i)) for _ in range(local)],
        out_shape=[jax.ShapeDtypeStruct((size, width), BF16) for _ in range(local)],
        scratch_shapes=[
            pltpu.VMEM((2, local * nodes // 2 * MAIN, total // 2), BF16),
            pltpu.VMEM((local * nodes * 2, total), BF16),
        ],
        compiler_params=pltpu.CompilerParams(vmem_limit_bytes=VMEM),
        cost_estimate=pl.CostEstimate(
            flops=4 * local * size * 256 * width, bytes_accessed=13_000_000, transcendentals=0
        ),
        name="part_rows",
    )(me, rows, rows)


def gathered_kernel(me_ref, rows_ref, ids_ref, out_ref, main_ref, tail_ref, *, tok, nodes, local):
    x, c = me_ref[0] // 2, me_ref[0] % 2
    chips = local // 2
    both = 2 * tok
    pair = 2 * MAIN
    per_node = local * CAP

    def chip_at(d):
        return (x + chips - d) % chips

    @pl.when(pl.program_id(0) == 0)
    def _():
        lane = iota((tok, EXTRA), 1)
        earlier = (iota((tok, tok), 1) < iota((tok, tok), 0)).astype(BF16)

        def place_of(source):
            ids = ids_ref[pl.ds(source * tok, tok), :].astype(F32)
            hit = jnp.zeros((tok, EXTRA), F32)
            for slot in range(TOP):
                hit = hit + (ids[:, slot : slot + 1] == (lane * local + me_ref[0]).astype(F32)).astype(F32)
            return jnp.where(hit > 0.5, dot(earlier, hit.astype(BF16)), -1.0).astype(BF16)

        shape = (nodes * pair, EXTRA)
        spread = (iota(shape, 0) // pair == iota(shape, 1)).astype(BF16)
        shape = (nodes * pair, both)
        row, at = iota(shape, 0), iota(shape, 1)
        core = at // tok
        main_fits = core == ((row % pair) // MAIN + c) % 2
        main_slot = (row % MAIN).astype(F32)
        tail_fits = core == ((row % pair) // 2 % 2 + c) % 2
        tail_slot = (MAIN + row % 2).astype(F32)
        for d in range(chips):
            a = chip_at(d)
            place = jnp.concatenate([place_of(2 * a), place_of(2 * a + 1)], axis=0)
            place = dot_nt(spread, place)
            main_ref[d] = jnp.logical_and(place == main_slot, main_fits).astype(BF16)
            here = jnp.logical_and(tail_fits, (row % pair) // 4 == d)
            tail_ref[d] = jnp.logical_and(place == tail_slot, here).astype(BF16)

    tail = None
    for d in range(chips):
        rows = rows_ref[pl.ds(pl.multiple_of(chip_at(d) * both, both), both), :]
        got = dot(main_ref[d], rows).astype(BF16)
        for n in range(nodes):
            out_ref[n * per_node + d * pair : n * per_node + (d + 1) * pair, :] = got[n * pair : (n + 1) * pair, :]
        part = dot(tail_ref[d], rows)
        tail = part if tail is None else tail + part
    tail = tail.astype(BF16)
    for n in range(nodes):
        out_ref[n * per_node + local * MAIN : (n + 1) * per_node, :] = tail[n * pair : (n + 1) * pair, :]


def gathered_rows(me, rows, nodes, local):
    total, wide = rows.shape
    width = wide - EXTRA
    tok = total // local
    fold = width // QUARTERS
    size = nodes * local * CAP
    pair = 2 * MAIN
    return pl.pallas_call(
        functools.partial(gathered_kernel, tok=tok, nodes=nodes, local=local),
        grid=(QUARTERS,),
        in_specs=[
            pl.BlockSpec(memory_space=pltpu.SMEM),
            pl.BlockSpec((total, fold), lambda i: (0, i)),
            pl.BlockSpec((total, EXTRA), lambda i: (0, width // EXTRA)),
        ],
        out_specs=pl.BlockSpec((size, fold), lambda i: (0, i)),
        out_shape=jax.ShapeDtypeStruct((size, width), BF16),
        scratch_shapes=[
            pltpu.VMEM((local // 2, nodes * pair, 2 * tok), BF16),
            pltpu.VMEM((local // 2, nodes * pair, 2 * tok), BF16),
        ],
        compiler_params=pltpu.CompilerParams(vmem_limit_bytes=VMEM),
        cost_estimate=pl.CostEstimate(
            flops=4 * size * 256 * width, bytes_accessed=17_000_000, transcendentals=0
        ),
        name="gathered_rows",
    )(me, rows, rows)


def pre_kernel(*refs, nodes, local):
    rows_refs, (w_ref, out_ref, rows_ref, made_ref, sems) = refs[:local], refs[local:]
    size = nodes * CAP
    per_node = local * CAP

    @pl.when(pl.program_id(0) == 0)
    def _():
        copies = [
            pltpu.make_async_copy(rows_refs[rel], rows_ref.at[pl.ds(rel * size, size), :], sems.at[rel])
            for rel in range(local)
        ]
        for copy in copies:
            copy.start()
        for copy in copies:
            copy.wait()

    made_ref[...] = dot(rows_ref[...], w_ref[...])
    for n in range(nodes):
        for rel in range(local):
            to, at = n * per_node + rel * MAIN, rel * size + n * MAIN
            out_ref[to : to + MAIN, :] = made_ref[at : at + MAIN, :]
            to, at = n * per_node + local * MAIN + rel * 2, rel * size + nodes * MAIN + n * 2
            out_ref[to : to + 2, :] = made_ref[at : at + 2, :]


def pre_of(parts, w_up, nodes, local, tile=256):
    width, hid = w_up.shape
    total = nodes * local * CAP
    return pl.pallas_call(
        functools.partial(pre_kernel, nodes=nodes, local=local),
        grid=(hid // tile,),
        in_specs=[pl.BlockSpec(memory_space=pl.ANY)] * local + [pl.BlockSpec((width, tile), lambda i: (0, i))],
        out_specs=pl.BlockSpec((total, tile), lambda i: (0, i)),
        out_shape=jax.ShapeDtypeStruct((total, hid), F32),
        scratch_shapes=[
            pltpu.VMEM((total, width), BF16),
            pltpu.VMEM((total, tile), F32),
            pltpu.SemaphoreType.DMA((local,)),
        ],
        compiler_params=pltpu.CompilerParams(vmem_limit_bytes=VMEM),
        cost_estimate=pl.CostEstimate(
            flops=2 * total * width * hid, bytes_accessed=22_000_000, transcendentals=0
        ),
        name="pre",
    )(*parts, w_up)


def back_kernel(
    me_ref, rows_ref, pre_ref, down_ref, up_ref, out_ref, raw_ref, inner_ref, gate_ref, piece_ref, stack_ref, fold_ref, extra_ref, sems, *, local
):
    step = pl.program_id(0)
    width = down_ref.shape[1]
    tile = down_ref.shape[0]
    hid = inner_ref.shape[1]
    main = out_ref.shape[0]
    fold = width // QUARTERS
    tails = 2 * GROUP
    size = GROUP * MAIN
    groups = main // size
    first = hid // tile

    for j in range(first):

        @pl.when(step == j)
        def _():
            pre = pre_ref[...]
            back = dot_nt(rows_ref[...], down_ref[...])
            sig = 1.0 / (1.0 + jnp.exp(-pre))
            act = (pre * sig).astype(BF16).astype(F32)
            raw_ref[:, j * tile : (j + 1) * tile] = (back * sig * (1.0 + pre * (1.0 - sig))).astype(BF16)
            gate = jnp.sum(act * back, axis=-1, keepdims=True)
            gate_ref[...] = gate if j == 0 else gate_ref[...] + gate

    def return_order():
        x, c = me_ref[0] // 2, me_ref[0] % 2
        rows = size + tails
        to, at = iota((rows, rows), 0), iota((rows, rows), 1)
        is_main = to < size
        source = jnp.where(is_main, to // MAIN, (to - size) // 2)
        node, place = source // local, source % local
        rel = ((x + local // 2 - place // 2) % (local // 2)) * 2 + (place + c) % 2
        start = jnp.where(is_main, rel * MAIN + to % MAIN, local * MAIN + rel * 2 + to % 2)
        return (at == node * (local * CAP) + start).astype(BF16)

    def copy_of(q):
        return pltpu.make_async_copy(
            piece_ref.at[q % 2], out_ref.at[:, pl.ds(q * fold, fold)], sems.at[q % 2]
        )

    fold_copy = pltpu.make_async_copy(fold_ref, out_ref.at[:, pl.ds(width, fold)], sems.at[2])
    extra_copy = pltpu.make_async_copy(extra_ref, out_ref.at[:, pl.ds(width + fold, EXTRA)], sems.at[3])

    for q in range(QUARTERS):

        @pl.when(step == first + q)
        def _():
            if q == 0:
                order = return_order()
                rows = size + tails
                for b in range(groups):
                    got = dot(order, raw_ref[b * rows : (b + 1) * rows, :]).astype(BF16)
                    inner_ref[b * size : (b + 1) * size, :] = got[:size, :]
                    inner_ref[main + b * tails : main + (b + 1) * tails, :] = got[size:, :]
            if q >= 2:
                copy_of(q - 2).wait()
            piece_ref[q % 2] = dot_nt(inner_ref[:main, :], up_ref[...]).astype(BF16)
            copy_of(q).start()
            if q == 0:
                pick = (iota((size, tails), 0) // MAIN == iota((size, tails), 1) // 2).astype(BF16)
                parity = iota((size, EXTRA), 0) % 2
                low = iota((size, EXTRA), 1) < EXTRA // 2
                for b in range(groups):
                    gates = jnp.broadcast_to(gate_ref[b * rows : (b + 1) * rows, :], (rows, EXTRA))
                    gates = dot(order, gates.astype(BF16))
                    mains, last = gates[:size, :], gates[size:, :]
                    odd = (iota((tails, EXTRA), 0) % 2 == 1)
                    even_rows = dot(pick, jnp.where(odd, 0.0, last).astype(BF16))
                    odd_rows = dot(pick, jnp.where(odd, last, 0.0).astype(BF16))
                    tail_rows = jnp.where(parity == 1, odd_rows, even_rows)
                    extra_ref[b * size : (b + 1) * size, :] = jnp.where(
                        low, mains, tail_rows
                    ).astype(BF16)
                extra_copy.start()
            piece = dot_nt(inner_ref[main:, :], up_ref[...]).astype(BF16)
            for b in range(groups):
                stack_ref[b * size + q * tails : b * size + (q + 1) * tails, :] = piece[b * tails : (b + 1) * tails, :]
            if q == QUARTERS - 1:
                to = iota((size, size), 0)
                source = ((to % MAIN) // 2) * tails + (to // MAIN) * 2 + to % 2
                order = (source == iota((size, size), 1)).astype(BF16)
                for b in range(groups):
                    fold_ref[b * size : (b + 1) * size, :] = dot(
                        order, stack_ref[b * size : (b + 1) * size, :]
                    ).astype(BF16)
                fold_copy.start()
                copy_of(q - 1).wait()
                copy_of(q).wait()
                extra_copy.wait()
                fold_copy.wait()


def pieces_of(me, rows, pre, w_down, w_up, local, tile=256):
    total, width = rows.shape
    hid = w_down.shape[0]
    main = total // CAP * MAIN
    fold = width // QUARTERS
    first = hid // tile
    return pl.pallas_call(
        functools.partial(back_kernel, local=local),
        grid=(first + QUARTERS,),
        in_specs=[
            pl.BlockSpec(memory_space=pltpu.SMEM),
            pl.BlockSpec((total, width), lambda i: (0, 0), pipeline_mode=pl.Buffered(1)),
            pl.BlockSpec((total, tile), lambda i: (0, jnp.minimum(i, first - 1))),
            pl.BlockSpec((tile, width), lambda i: (jnp.minimum(i, first - 1), 0)),
            pl.BlockSpec((fold, hid), lambda i: (jnp.maximum(i - first, 0), 0)),
        ],
        out_specs=pl.BlockSpec(memory_space=pl.ANY),
        out_shape=jax.ShapeDtypeStruct((main, width + fold + EXTRA), BF16),
        scratch_shapes=[
            pltpu.VMEM((total, hid), BF16),
            pltpu.VMEM((total, hid), BF16),
            pltpu.VMEM((total, 1), F32),
            pltpu.VMEM((2, main, fold), BF16),
            pltpu.VMEM((main, fold), BF16),
            pltpu.VMEM((main, fold), BF16),
            pltpu.VMEM((main, EXTRA), BF16),
            pltpu.SemaphoreType.DMA((4,)),
        ],
        compiler_params=pltpu.CompilerParams(vmem_limit_bytes=VMEM),
        cost_estimate=pl.CostEstimate(
            flops=4 * total * width * hid, bytes_accessed=39_000_000, transcendentals=total * hid
        ),
        name="back_and_pieces",
    )(me, rows, pre, w_down, w_up)


def combine_kernel(ids_ref, gate_ref, rows_ref, out_ref, grad_ref, acc_ref, sum_ref):
    step = pl.program_id(0)
    tok, width = out_ref.shape
    fold = width // QUARTERS
    ids = ids_ref[...]
    main, tail, quarter, spread, expert = picks(ids, step * GROUP)
    high = jnp.zeros(expert.shape, F32)
    low = jnp.zeros(expert.shape, F32)
    for slot in range(ids.shape[0]):
        same = expert == ids[slot : slot + 1, :]
        fixed = gate_ref[slot : slot + 1, :]
        high = high + jnp.where(same, (fixed // 256).astype(F32), 0.0)
        low = low + jnp.where(same, (fixed % 256).astype(F32), 0.0)
    high = dot(spread, high.astype(BF16)) * (1.0 / 256.0)
    low = dot(spread, low.astype(BF16)) * (1.0 / 65536.0)

    def weights(mask):
        return jnp.concatenate([jnp.where(mask, high, 0.0), jnp.where(mask, low, 0.0)], axis=1).astype(BF16)

    @pl.when(step == 0)
    def _():
        acc_ref[...] = jnp.zeros_like(acc_ref)
        sum_ref[...] = jnp.zeros_like(sum_ref)

    both = dot_tn(weights(main), rows_ref[:, :width])
    acc_ref[...] += both[:tok, :] + both[tok:, :]
    for q in range(QUARTERS):
        both = dot_tn(weights(jnp.logical_and(tail, quarter == q)), rows_ref[:, width : width + fold])
        acc_ref[:, q * fold : (q + 1) * fold] += both[:tok, :] + both[tok:, :]

    extra = rows_ref[:, width + fold :].astype(F32)
    value = jnp.where(main, extra[:, 0:1], 0.0) + jnp.where(
        jnp.logical_and(tail, quarter == 0), extra[:, EXTRA // 2 : EXTRA // 2 + 1], 0.0
    )
    value = dot_tn(spread, value.astype(BF16))
    for slot in range(ids.shape[0]):
        part = jnp.sum(jnp.where(expert == ids[slot : slot + 1, :], value, 0.0), axis=0, keepdims=True)
        sum_ref[slot : slot + 1, :] = sum_ref[slot : slot + 1, :] + part

    @pl.when(step == pl.num_programs(0) - 1)
    def _():
        out_ref[...] = acc_ref[...].astype(BF16)
        grad_ref[...] = sum_ref[...]


def combine(ids_t, gate_t, rows, width):
    top, tok = ids_t.shape
    main, wide = rows.shape
    size = GROUP * MAIN
    return pl.pallas_call(
        combine_kernel,
        grid=(main // size,),
        in_specs=[
            pl.BlockSpec((top, tok), lambda i: (0, 0)),
            pl.BlockSpec((top, tok), lambda i: (0, 0)),
            pl.BlockSpec((size, wide), lambda i: (i, 0)),
        ],
        out_specs=[
            pl.BlockSpec((tok, width), lambda i: (0, 0)),
            pl.BlockSpec((top, tok), lambda i: (0, 0)),
        ],
        out_shape=[
            jax.ShapeDtypeStruct((tok, width), BF16),
            jax.ShapeDtypeStruct((top, tok), F32),
        ],
        scratch_shapes=[pltpu.VMEM((tok, width), F32), pltpu.VMEM((top, tok), F32)],
        compiler_params=pltpu.CompilerParams(vmem_limit_bytes=VMEM),
        name="combine",
    )(ids_t, gate_t, rows)


def exchange(rows, axes):
    count = lax.axis_size(axes)
    blocks = rows.reshape(count, rows.shape[0] // count, rows.shape[1])
    blocks = lax.all_to_all(blocks, axes, split_axis=0, concat_axis=0, tiled=True)
    return blocks.reshape(rows.shape)


def shift(rows, rel, local):
    chips = local // 2
    pairs = [(2 * x + c, 2 * ((x + rel // 2) % chips) + (c + rel) % 2) for x in range(chips) for c in range(2)]
    return lax.ppermute(rows, "local", pairs)


def per_device(tokens, cotangent, expert_ids, gate_fixed, w_up, w_down):
    nodes, local = lax.axis_size("node"), lax.axis_size("local")
    width = tokens.shape[1]
    ids_t = expert_ids.T
    gate_t = gate_fixed.T
    me = lax.axis_index("local").astype(jnp.int32).reshape(1)
    marked = jnp.concatenate(
        [cotangent, jnp.pad(expert_ids.astype(BF16), ((0, 0), (0, EXTRA - expert_ids.shape[1])))], axis=1
    )
    rows_dy = lax.all_gather(marked, "local", tiled=True)
    rows_x = exchange(node_rows(ids_t, tokens, nodes, local), "node")
    rows_dy = exchange(gathered_rows(me, rows_dy, nodes, local), "node")
    parts = part_rows(me, rows_x, nodes, local)
    parts = [parts[0]] + [shift(parts[rel], rel, local) for rel in range(1, local)]
    pre = pre_of(parts, w_up[0], nodes, local)
    pieces = pieces_of(me, rows_dy, pre, w_down[0], w_up[0], local)
    grad_input, grad_gate = combine(ids_t, gate_t, exchange(pieces, ("node", "local")), width)
    return grad_input, grad_gate.T.astype(BF16)


def solution(mesh):
    split = P(("node", "local"), None)
    experts = P(("node", "local"), None, None)
    return jax.shard_map(
        per_device,
        mesh=mesh,
        in_specs=(split, split, split, split, experts, experts),
        out_specs=(split, split),
        check_vma=False,
    )
```

```python
import functools

import jax
import jax.numpy as jnp
from jax import lax
from jax.experimental import pallas as pl
from jax.experimental.pallas import tpu as pltpu
from jax.sharding import PartitionSpec as P

TOP = 8
NODES_MAX = 4
CAP = 10
MAIN = 8
QUARTERS = 4
GROUP = 32
EXTRA = 128
VMEM = 56 * 1024 * 1024
BF16 = jnp.bfloat16
F32 = jnp.float32


def iota(shape, dim):
    return lax.broadcasted_iota(jnp.int32, shape, dim)


def dot(a, b):
    return jnp.dot(a, b, preferred_element_type=F32)


def dot_nt(a, b):
    return lax.dot_general(a, b, (((1,), (1,)), ((), ())), preferred_element_type=F32)


def dot_tn(a, b):
    return lax.dot_general(a, b, (((0,), (0,)), ((), ())), preferred_element_type=F32)


def places(ids, first, count):
    tok = ids.shape[1]
    expert = first + iota((count, tok), 0)
    hit = jnp.zeros((count, tok), F32)
    for slot in range(ids.shape[0]):
        hit = hit + (expert == ids[slot : slot + 1, :]).astype(F32)
    earlier = (iota((tok, tok), 0) < iota((tok, tok), 1)).astype(BF16)
    return jnp.where(hit > 0.5, dot(hit.astype(BF16), earlier), -1.0), expert


def node_kernel(ids_ref, x_ref, dy_ref, out_ref, marked_ref, *, share, nodes, local):
    width = x_ref.shape[1]
    tok = x_ref.shape[0]
    rows = out_ref.shape[0]
    some = rows // share
    ids = ids_ref[...]
    first = pl.program_id(0) * some
    node = first + iota((some, tok), 0)
    named = jnp.zeros((some, tok), F32)
    for slot in range(ids.shape[0]):
        named = jnp.maximum(named, (node == ids[slot : slot + 1, :] // local).astype(F32))
    earlier = (iota((tok, tok), 0) < iota((tok, tok), 1)).astype(BF16)
    rank = jnp.where(named > 0.5, dot(named.astype(BF16), earlier), -1.0)
    spread = (iota((rows, some), 0) // share == iota((rows, some), 1)).astype(BF16)
    wanted = (iota((rows, tok), 0) % share).astype(F32)
    pick = (dot(spread, rank.astype(BF16)) == wanted).astype(BF16)
    out_ref[:, :width] = dot(pick, x_ref[...]).astype(BF16)
    count = some * local
    place, _ = places(ids, first * local, count)
    slots = dot_nt(pick, place.astype(BF16))
    slots = jnp.where(iota((rows, count), 0) // share == iota((rows, count), 1) // local, slots, 0.0)
    lanes = (iota((count, EXTRA), 0) % local == iota((count, EXTRA), 1)).astype(BF16)
    out_ref[:, width:] = dot(slots.astype(BF16), lanes).astype(BF16)
    own = iota((ids.shape[0], EXTRA), 0) == iota((ids.shape[0], EXTRA), 1)
    marked_ref[:, :width] = dy_ref[...]
    part = marked_ref.shape[0]
    here = (iota((part, tok), 0) + pl.program_id(0) * part == iota((part, tok), 1)).astype(BF16)
    by_token = dot_tn(ids.astype(F32).astype(BF16), own.astype(BF16)).astype(BF16)
    marked_ref[:, width:] = dot(here, by_token).astype(BF16)


def node_rows(ids_t, x, dy, nodes, local):
    top, tok = ids_t.shape
    width = x.shape[1]
    share = tok * NODES_MAX // nodes
    steps = 4
    part = tok // steps
    return pl.pallas_call(
        functools.partial(node_kernel, share=share, nodes=nodes, local=local),
        grid=(steps,),
        in_specs=[
            pl.BlockSpec((top, tok), lambda i: (0, 0)),
            pl.BlockSpec((tok, width), lambda i: (0, 0)),
            pl.BlockSpec((part, width), lambda i: (i, 0)),
        ],
        out_specs=[
            pl.BlockSpec((nodes * share // steps, width + EXTRA), lambda i: (i, 0)),
            pl.BlockSpec((part, width + EXTRA), lambda i: (i, 0)),
        ],
        out_shape=[
            jax.ShapeDtypeStruct((nodes * share, width + EXTRA), BF16),
            jax.ShapeDtypeStruct((tok, width + EXTRA), BF16),
        ],
        compiler_params=pltpu.CompilerParams(vmem_limit_bytes=VMEM),
        cost_estimate=pl.CostEstimate(
            flops=2 * nodes * share * 256 * width, bytes_accessed=7_000_000, transcendentals=0
        ),
        name="node_rows",
    )(ids_t, x, dy)


def part_kernel(me_ref, rows_ref, slots_ref, *refs, share, nodes, local):
    outs, (main_ref, tail_ref) = refs[:local], refs[local:]
    x, c = me_ref[0] // 2, me_ref[0] % 2
    half = nodes // 2
    rows = half * share
    mains = half * MAIN
    tails = 2 * nodes

    def to_of(rel):
        return ((x + rel // 2) % (local // 2)) * 2 + (c + rel) % 2

    @pl.when(pl.program_id(0) == 0)
    def _():
        col, lane = iota((local * mains, EXTRA), 0), iota((local * mains, EXTRA), 1)
        spread = (lane == to_of(col // mains)).astype(BF16)
        shape = (local * mains, rows)
        row, at = iota(shape, 0), iota(shape, 1)
        fits = at // share == (row % mains) // MAIN
        slot = (row % MAIN).astype(F32)
        for g in range(2):
            place = dot_nt(spread, slots_ref[g * rows : (g + 1) * rows, :])
            main_ref[g] = jnp.logical_and(place == slot, fits).astype(BF16)
        col, lane = iota((local * tails, EXTRA), 0), iota((local * tails, EXTRA), 1)
        spread = (lane == to_of(col // tails)).astype(BF16)
        shape = (local * tails, 2 * rows)
        row, at = iota(shape, 0), iota(shape, 1)
        place = dot_nt(spread, slots_ref[...])
        fits = at // share == (row % tails) // 2
        tail_ref[...] = jnp.logical_and(place == (MAIN + row % 2).astype(F32), fits).astype(BF16)

    for g in range(2):
        got = dot(main_ref[g], rows_ref[g * rows : (g + 1) * rows, :]).astype(BF16)
        for rel in range(local):
            outs[rel][g * mains : (g + 1) * mains, :] = got[rel * mains : (rel + 1) * mains, :]
    got = dot(tail_ref[...], rows_ref[...]).astype(BF16)
    for rel in range(local):
        outs[rel][2 * mains :, :] = got[rel * tails : (rel + 1) * tails, :]


def part_rows(me, rows, nodes, local):
    total, wide = rows.shape
    width = wide - EXTRA
    share = total // nodes
    fold = width // QUARTERS
    size = nodes * CAP
    return pl.pallas_call(
        functools.partial(part_kernel, share=share, nodes=nodes, local=local),
        grid=(QUARTERS,),
        in_specs=[
            pl.BlockSpec(memory_space=pltpu.SMEM),
            pl.BlockSpec((total, fold), lambda i: (0, i)),
            pl.BlockSpec((total, EXTRA), lambda i: (0, width // EXTRA)),
        ],
        out_specs=[pl.BlockSpec((size, fold), lambda i: (0, i)) for _ in range(local)],
        out_shape=[jax.ShapeDtypeStruct((size, width), BF16) for _ in range(local)],
        scratch_shapes=[
            pltpu.VMEM((2, local * nodes // 2 * MAIN, total // 2), BF16),
            pltpu.VMEM((local * nodes * 2, total), BF16),
        ],
        compiler_params=pltpu.CompilerParams(vmem_limit_bytes=VMEM),
        cost_estimate=pl.CostEstimate(
            flops=4 * local * size * 256 * width, bytes_accessed=13_000_000, transcendentals=0
        ),
        name="part_rows",
    )(me, rows, rows)


def gathered_kernel(me_ref, *refs, tok, nodes, local):
    rows_refs, ids_refs, (out_ref, main_ref, tail_ref) = refs[:local], refs[local : 2 * local], refs[2 * local :]
    pair = 2 * MAIN
    per_node = local * CAP

    @pl.when(pl.program_id(0) == 0)
    def _():
        lane = iota((tok, EXTRA), 1)
        earlier = (iota((tok, tok), 1) < iota((tok, tok), 0)).astype(BF16)

        def place_of(ids_ref):
            ids = ids_ref[...].astype(F32)
            hit = jnp.zeros((tok, EXTRA), F32)
            for slot in range(TOP):
                hit = hit + (ids[:, slot : slot + 1] == (lane * local + me_ref[0]).astype(F32)).astype(F32)
            return jnp.where(hit > 0.5, dot(earlier, hit.astype(BF16)), -1.0).astype(BF16)

        shape = (nodes * pair, EXTRA)
        spread = (iota(shape, 0) // pair == iota(shape, 1)).astype(BF16)
        shape = (nodes * pair, 2 * tok)
        row, at = iota(shape, 0), iota(shape, 1)
        core = at // tok
        main_fits = core == (row % pair) // MAIN
        main_slot = (row % MAIN).astype(F32)
        tail_fits = core == (row % pair) // 2 % 2
        tail_slot = (MAIN + row % 2).astype(F32)
        for d in range(local // 2):
            place = jnp.concatenate([place_of(ids_refs[2 * d]), place_of(ids_refs[2 * d + 1])], axis=0)
            place = dot_nt(spread, place)
            main_ref[d] = jnp.logical_and(place == main_slot, main_fits).astype(BF16)
            here = jnp.logical_and(tail_fits, (row % pair) // 4 == d)
            tail_ref[d] = jnp.logical_and(place == tail_slot, here).astype(BF16)

    tail = None
    for d in range(local // 2):
        rows = jnp.concatenate([rows_refs[2 * d][...], rows_refs[2 * d + 1][...]], axis=0)
        got = dot(main_ref[d], rows).astype(BF16)
        for n in range(nodes):
            out_ref[n * per_node + d * pair : n * per_node + (d + 1) * pair, :] = got[n * pair : (n + 1) * pair, :]
        part = dot(tail_ref[d], rows)
        tail = part if tail is None else tail + part
    tail = tail.astype(BF16)
    for n in range(nodes):
        out_ref[n * per_node + local * MAIN : (n + 1) * per_node, :] = tail[n * pair : (n + 1) * pair, :]


def gathered_rows(me, parts, nodes, local):
    tok, wide = parts[0].shape
    width = wide - EXTRA
    tile = width // 7
    size = nodes * local * CAP
    picks = pltpu.VMEM((local // 2, nodes * 2 * MAIN, 2 * tok), BF16)
    return pl.pallas_call(
        functools.partial(gathered_kernel, tok=tok, nodes=nodes, local=local),
        grid=(width // tile,),
        in_specs=[pl.BlockSpec(memory_space=pltpu.SMEM)]
        + [pl.BlockSpec((tok, tile), lambda i: (0, i))] * local
        + [pl.BlockSpec((tok, EXTRA), lambda i: (0, width // EXTRA))] * local,
        out_specs=pl.BlockSpec((size, tile), lambda i: (0, i)),
        out_shape=jax.ShapeDtypeStruct((size, width), BF16),
        scratch_shapes=[picks, picks],
        compiler_params=pltpu.CompilerParams(vmem_limit_bytes=VMEM),
        cost_estimate=pl.CostEstimate(
            flops=4 * size * 256 * width, bytes_accessed=17_000_000, transcendentals=0
        ),
        name="gathered_rows",
    )(me, *parts, *parts)


def pre_kernel(*refs, nodes):
    rows_refs, (w_ref, out_ref, rows_ref, made_ref, sems) = refs[:-5], refs[-5:]
    count = len(rows_refs)
    size = nodes * CAP
    per_node = count * CAP

    @pl.when(pl.program_id(0) == 0)
    def _():
        copies = [
            pltpu.make_async_copy(rows_refs[i], rows_ref.at[pl.ds(i * size, size), :], sems.at[i])
            for i in range(count)
        ]
        for copy in copies:
            copy.start()
        for copy in copies:
            copy.wait()

    made_ref[...] = dot(rows_ref[...], w_ref[...])
    for n in range(nodes):
        for i in range(count):
            to, at = n * per_node + i * MAIN, i * size + n * MAIN
            out_ref[to : to + MAIN, :] = made_ref[at : at + MAIN, :]
            to, at = n * per_node + count * MAIN + i * 2, i * size + nodes * MAIN + n * 2
            out_ref[to : to + 2, :] = made_ref[at : at + 2, :]


def pre_of(parts, w_up, nodes, tile=256):
    width, hid = w_up.shape
    count = len(parts)
    total = nodes * count * CAP
    return pl.pallas_call(
        functools.partial(pre_kernel, nodes=nodes),
        grid=(hid // tile,),
        in_specs=[pl.BlockSpec(memory_space=pl.ANY)] * count + [pl.BlockSpec((width, tile), lambda i: (0, i))],
        out_specs=pl.BlockSpec((total, tile), lambda i: (0, i)),
        out_shape=jax.ShapeDtypeStruct((total, hid), F32),
        scratch_shapes=[
            pltpu.VMEM((total, width), BF16),
            pltpu.VMEM((total, tile), F32),
            pltpu.SemaphoreType.DMA((count,)),
        ],
        compiler_params=pltpu.CompilerParams(vmem_limit_bytes=VMEM),
        cost_estimate=pl.CostEstimate(
            flops=2 * total * width * hid, bytes_accessed=15_000_000, transcendentals=0
        ),
        name="pre",
    )(*parts, w_up)


def back_kernel(
    me_ref, rows_ref, early_ref, late_ref, down_ref, up_ref, out_ref, raw_ref, inner_ref, gate_ref, piece_ref, stack_ref, fold_ref, extra_ref, sems, pre_ref, *, local
):
    step = pl.program_id(0)
    width = down_ref.shape[1]
    tile = down_ref.shape[0]
    hid = inner_ref.shape[1]
    main = out_ref.shape[0]
    fold = width // QUARTERS
    tails = 2 * GROUP
    size = GROUP * MAIN
    groups = main // size
    first = hid // tile

    for j in range(first):

        @pl.when(step == j)
        def _():
            mains, lasts = local // 2 * MAIN, local // 2 * 2
            half = mains + lasts
            for n in range(main // (local * MAIN)):
                for h, ref in enumerate((early_ref, late_ref)):
                    to = n * 2 * half + h * mains
                    pre_ref[to : to + mains, :] = ref[n * half : n * half + mains, :]
                    to = n * 2 * half + 2 * mains + h * lasts
                    pre_ref[to : to + lasts, :] = ref[n * half + mains : (n + 1) * half, :]
            pre = pre_ref[...]
            back = dot_nt(rows_ref[...], down_ref[...])
            sig = 1.0 / (1.0 + jnp.exp(-pre))
            act = (pre * sig).astype(BF16).astype(F32)
            raw_ref[:, j * tile : (j + 1) * tile] = (back * sig * (1.0 + pre * (1.0 - sig))).astype(BF16)
            gate = jnp.sum(act * back, axis=-1, keepdims=True)
            gate_ref[...] = gate if j == 0 else gate_ref[...] + gate

    def return_order():
        x, c = me_ref[0] // 2, me_ref[0] % 2
        rows = size + tails
        to, at = iota((rows, rows), 0), iota((rows, rows), 1)
        is_main = to < size
        source = jnp.where(is_main, to // MAIN, (to - size) // 2)
        node, place = source // local, source % local
        rel = ((x + local // 2 - place // 2) % (local // 2)) * 2 + (place + c) % 2
        start = jnp.where(is_main, rel * MAIN + to % MAIN, local * MAIN + rel * 2 + to % 2)
        return (at == node * (local * CAP) + start).astype(BF16)

    def copy_of(q):
        return pltpu.make_async_copy(
            piece_ref.at[q % 2], out_ref.at[:, pl.ds(q * fold, fold)], sems.at[q % 2]
        )

    fold_copy = pltpu.make_async_copy(fold_ref, out_ref.at[:, pl.ds(width, fold)], sems.at[2])
    extra_copy = pltpu.make_async_copy(extra_ref, out_ref.at[:, pl.ds(width + fold, EXTRA)], sems.at[3])

    for q in range(QUARTERS):

        @pl.when(step == first + q)
        def _():
            if q == 0:
                order = return_order()
                rows = size + tails
                for b in range(groups):
                    got = dot(order, raw_ref[b * rows : (b + 1) * rows, :]).astype(BF16)
                    inner_ref[b * size : (b + 1) * size, :] = got[:size, :]
                    inner_ref[main + b * tails : main + (b + 1) * tails, :] = got[size:, :]
            if q >= 2:
                copy_of(q - 2).wait()
            piece_ref[q % 2] = dot_nt(inner_ref[:main, :], up_ref[...]).astype(BF16)
            copy_of(q).start()
            if q == 0:
                pick = (iota((size, tails), 0) // MAIN == iota((size, tails), 1) // 2).astype(BF16)
                parity = iota((size, EXTRA), 0) % 2
                low = iota((size, EXTRA), 1) < EXTRA // 2
                for b in range(groups):
                    gates = jnp.broadcast_to(gate_ref[b * rows : (b + 1) * rows, :], (rows, EXTRA))
                    gates = dot(order, gates.astype(BF16))
                    mains, last = gates[:size, :], gates[size:, :]
                    odd = (iota((tails, EXTRA), 0) % 2 == 1)
                    even_rows = dot(pick, jnp.where(odd, 0.0, last).astype(BF16))
                    odd_rows = dot(pick, jnp.where(odd, last, 0.0).astype(BF16))
                    tail_rows = jnp.where(parity == 1, odd_rows, even_rows)
                    extra_ref[b * size : (b + 1) * size, :] = jnp.where(
                        low, mains, tail_rows
                    ).astype(BF16)
                extra_copy.start()
            piece = dot_nt(inner_ref[main:, :], up_ref[...]).astype(BF16)
            for b in range(groups):
                stack_ref[b * size + q * tails : b * size + (q + 1) * tails, :] = piece[b * tails : (b + 1) * tails, :]
            if q == QUARTERS - 1:
                to = iota((size, size), 0)
                source = ((to % MAIN) // 2) * tails + (to // MAIN) * 2 + to % 2
                order = (source == iota((size, size), 1)).astype(BF16)
                for b in range(groups):
                    fold_ref[b * size : (b + 1) * size, :] = dot(
                        order, stack_ref[b * size : (b + 1) * size, :]
                    ).astype(BF16)
                fold_copy.start()
                copy_of(q - 1).wait()
                copy_of(q).wait()
                extra_copy.wait()
                fold_copy.wait()


def pieces_of(me, rows, early, late, w_down, w_up, local, tile=256):
    total, width = rows.shape
    hid = w_down.shape[0]
    main = total // CAP * MAIN
    fold = width // QUARTERS
    first = hid // tile
    return pl.pallas_call(
        functools.partial(back_kernel, local=local),
        grid=(first + QUARTERS,),
        in_specs=[
            pl.BlockSpec(memory_space=pltpu.SMEM),
            pl.BlockSpec((total, width), lambda i: (0, 0), pipeline_mode=pl.Buffered(1)),
            pl.BlockSpec((total // 2, tile), lambda i: (0, jnp.minimum(i, first - 1))),
            pl.BlockSpec((total // 2, tile), lambda i: (0, jnp.minimum(i, first - 1))),
            pl.BlockSpec((tile, width), lambda i: (jnp.minimum(i, first - 1), 0)),
            pl.BlockSpec((fold, hid), lambda i: (jnp.maximum(i - first, 0), 0)),
        ],
        out_specs=pl.BlockSpec(memory_space=pl.ANY),
        out_shape=jax.ShapeDtypeStruct((main, width + fold + EXTRA), BF16),
        scratch_shapes=[
            pltpu.VMEM((total, hid), BF16),
            pltpu.VMEM((total, hid), BF16),
            pltpu.VMEM((total, 1), F32),
            pltpu.VMEM((2, main, fold), BF16),
            pltpu.VMEM((main, fold), BF16),
            pltpu.VMEM((main, fold), BF16),
            pltpu.VMEM((main, EXTRA), BF16),
            pltpu.SemaphoreType.DMA((4,)),
            pltpu.VMEM((total, tile), F32),
        ],
        compiler_params=pltpu.CompilerParams(vmem_limit_bytes=VMEM),
        cost_estimate=pl.CostEstimate(
            flops=4 * total * width * hid, bytes_accessed=39_000_000, transcendentals=total * hid
        ),
        name="back_and_pieces",
    )(me, rows, early, late, w_down, w_up)


def combine_kernel(ids_ref, gate_ref, rows_ref, fold_ref, extra_ref, out_ref, grad_ref, main_ref, last_ref, tail_ref):
    step = pl.program_id(0)
    top, tok = ids_ref.shape
    fold = fold_ref.shape[1]
    size = GROUP * MAIN
    tails = 2 * GROUP
    groups = rows_ref.shape[0] // size

    @pl.when(step == 0)
    def _():
        ids = ids_ref[...]
        to = iota((size, size), 0)
        unfold = ((to % tails) // 2) * MAIN + (to // tails) * 2 + to % 2
        unfold = (unfold == iota((size, size), 1)).astype(BF16)
        spread = (iota((size, GROUP), 0) // MAIN == iota((size, GROUP), 1)).astype(BF16)
        twice = (iota((tails, GROUP), 0) // 2 == iota((tails, GROUP), 1)).astype(BF16)
        row, last_row = iota((size, tok), 0), iota((tails, tok), 0)
        grads = [jnp.zeros((1, tok), F32) for _ in range(top)]
        for b in range(groups):
            place, expert = places(ids, b * GROUP, GROUP)
            place = place.astype(BF16)
            high = jnp.zeros(expert.shape, F32)
            low = jnp.zeros(expert.shape, F32)
            for slot in range(top):
                same = expert == ids[slot : slot + 1, :]
                fixed = gate_ref[slot : slot + 1, :]
                high = high + jnp.where(same, (fixed // 256).astype(F32), 0.0)
                low = low + jnp.where(same, (fixed % 256).astype(F32), 0.0)
            gates = jnp.concatenate([high, low], axis=1).astype(BF16)

            def weights(copies, slots):
                mask = dot(copies, place) == slots.astype(F32)
                both = dot(copies, gates)
                scaled = [both[:, :tok] * (1.0 / 256.0), both[:, tok:] * (1.0 / 65536.0)]
                return mask, jnp.concatenate([jnp.where(mask, part, 0.0) for part in scaled], axis=1)

            main, weight = weights(spread, row % MAIN)
            main_ref[:, b * size : (b + 1) * size] = weight.T.astype(BF16)
            tail, weight = weights(twice, MAIN + last_row % 2)
            last_ref[:, b * tails : (b + 1) * tails] = weight.T.astype(BF16)
            stack = dot(unfold, fold_ref[b * size : (b + 1) * size, :]).astype(BF16)
            for q in range(QUARTERS):
                tail_ref[q, b * tails : (b + 1) * tails, :] = stack[q * tails : (q + 1) * tails, :]
            extra = extra_ref[b * size : (b + 1) * size, :]
            value = jnp.where(main, extra[:, 0:1].astype(F32), 0.0)
            last = dot(unfold[:tails, :], extra)[:, EXTRA // 2 : EXTRA // 2 + 1]
            last = jnp.where(tail, last, 0.0)
            value = dot_tn(spread, value.astype(BF16)) + dot_tn(twice, last.astype(BF16))
            for slot in range(top):
                same = expert == ids[slot : slot + 1, :]
                grads[slot] = grads[slot] + jnp.sum(jnp.where(same, value, 0.0), axis=0, keepdims=True)
        grad_ref[...] = jnp.concatenate(grads, axis=0).astype(BF16)

    both = dot(main_ref[...], rows_ref[...]) + dot(last_ref[...], tail_ref[step])
    out_ref[...] = (both[:tok, :] + both[tok:, :]).astype(BF16)


def combine(ids_t, gate_t, rows, width):
    top, tok = ids_t.shape
    main, wide = rows.shape
    fold = width // QUARTERS
    tails = main // QUARTERS
    return pl.pallas_call(
        combine_kernel,
        grid=(QUARTERS,),
        in_specs=[
            pl.BlockSpec((top, tok), lambda i: (0, 0)),
            pl.BlockSpec((top, tok), lambda i: (0, 0)),
            pl.BlockSpec((main, fold), lambda i: (0, i)),
            pl.BlockSpec((main, fold), lambda i: (0, QUARTERS)),
            pl.BlockSpec((main, EXTRA), lambda i: (0, (width + fold) // EXTRA)),
        ],
        out_specs=[
            pl.BlockSpec((tok, fold), lambda i: (0, i)),
            pl.BlockSpec((top, tok), lambda i: (0, 0)),
        ],
        out_shape=[
            jax.ShapeDtypeStruct((tok, width), BF16),
            jax.ShapeDtypeStruct((top, tok), BF16),
        ],
        scratch_shapes=[
            pltpu.VMEM((2 * tok, main), BF16),
            pltpu.VMEM((2 * tok, tails), BF16),
            pltpu.VMEM((QUARTERS, tails, fold), BF16),
        ],
        compiler_params=pltpu.CompilerParams(vmem_limit_bytes=VMEM),
        name="combine",
    )(ids_t, gate_t, rows, rows, rows)


def exchange(rows, axes):
    count = lax.axis_size(axes)
    blocks = rows.reshape(count, rows.shape[0] // count, rows.shape[1])
    blocks = lax.all_to_all(blocks, axes, split_axis=0, concat_axis=0, tiled=True)
    return blocks.reshape(rows.shape)


def shift(rows, rel, local):
    chips = local // 2
    pairs = [(2 * x + c, 2 * ((x + rel // 2) % chips) + (c + rel) % 2) for x in range(chips) for c in range(2)]
    return lax.ppermute(rows, "local", pairs)


def per_device(tokens, cotangent, expert_ids, gate_fixed, w_up, w_down):
    nodes, local = lax.axis_size("node"), lax.axis_size("local")
    width = tokens.shape[1]
    ids_t = expert_ids.T
    gate_t = gate_fixed.T
    me = lax.axis_index("local").astype(jnp.int32).reshape(1)
    send_x, marked = node_rows(ids_t, tokens, cotangent, nodes, local)
    rows_x = exchange(send_x, "node")
    same = [marked] + [shift(marked, 2 * d, local) for d in range(1, local // 2)]
    all_dy = [part for rows in same for part in (rows, shift(rows, 1, local))]
    rows_dy = exchange(gathered_rows(me, all_dy, nodes, local), "node")
    parts = part_rows(me, rows_x, nodes, local)
    parts = [parts[0]] + [shift(parts[rel], rel, local) for rel in range(1, local)]
    early = pre_of(parts[: local // 2], w_up[0], nodes)
    late = pre_of(parts[local // 2 :], w_up[0], nodes)
    pieces = pieces_of(me, rows_dy, early, late, w_down[0], w_up[0], local)
    grad_input, grad_gate = combine(ids_t, gate_t, exchange(pieces, ("node", "local")), width)
    return grad_input, grad_gate.T


def solution(mesh):
    split = P(("node", "local"), None)
    experts = P(("node", "local"), None, None)
    return jax.shard_map(
        per_device,
        mesh=mesh,
        in_specs=(split, split, split, split, experts, experts),
        out_specs=(split, split),
        check_vma=False,
    )
```

```python
import functools

import jax
import jax.numpy as jnp
from jax import lax
from jax.experimental import pallas as pl
from jax.experimental.pallas import tpu as pltpu
from jax.sharding import PartitionSpec as P

TOP = 8
NODES_MAX = 4
CAP = 10
MAIN = 8
QUARTERS = 4
GROUP = 32
EXTRA = 128
VMEM = 56 * 1024 * 1024
BF16 = jnp.bfloat16
F32 = jnp.float32


def iota(shape, dim):
    return lax.broadcasted_iota(jnp.int32, shape, dim)


def dot(a, b):
    return jnp.dot(a, b, preferred_element_type=F32)


def dot_nt(a, b):
    return lax.dot_general(a, b, (((1,), (1,)), ((), ())), preferred_element_type=F32)


def dot_tn(a, b):
    return lax.dot_general(a, b, (((0,), (0,)), ((), ())), preferred_element_type=F32)


def places(ids, first, count):
    tok = ids.shape[1]
    expert = first + iota((count, tok), 0)
    hit = jnp.zeros((count, tok), F32)
    for slot in range(ids.shape[0]):
        hit = hit + (expert == ids[slot : slot + 1, :]).astype(F32)
    earlier = (iota((tok, tok), 0) < iota((tok, tok), 1)).astype(BF16)
    return jnp.where(hit > 0.5, dot(hit.astype(BF16), earlier), -1.0), expert


def node_kernel(ids_ref, x_ref, dy_ref, out_ref, marked_ref, *, share, nodes, local):
    width = x_ref.shape[1]
    tok = x_ref.shape[0]
    rows = out_ref.shape[0]
    some = rows // share
    ids = ids_ref[...]
    first = pl.program_id(0) * some
    node = first + iota((some, tok), 0)
    named = jnp.zeros((some, tok), F32)
    for slot in range(ids.shape[0]):
        named = jnp.maximum(named, (node == ids[slot : slot + 1, :] // local).astype(F32))
    earlier = (iota((tok, tok), 0) < iota((tok, tok), 1)).astype(BF16)
    rank = jnp.where(named > 0.5, dot(named.astype(BF16), earlier), -1.0)
    spread = (iota((rows, some), 0) // share == iota((rows, some), 1)).astype(BF16)
    wanted = (iota((rows, tok), 0) % share).astype(F32)
    pick = (dot(spread, rank.astype(BF16)) == wanted).astype(BF16)
    out_ref[:, :width] = dot(pick, x_ref[...]).astype(BF16)
    count = some * local
    place, _ = places(ids, first * local, count)
    slots = dot_nt(pick, place.astype(BF16))
    slots = jnp.where(iota((rows, count), 0) // share == iota((rows, count), 1) // local, slots, 0.0)
    lanes = (iota((count, EXTRA), 0) % local == iota((count, EXTRA), 1)).astype(BF16)
    out_ref[:, width:] = dot(slots.astype(BF16), lanes).astype(BF16)
    own = iota((ids.shape[0], EXTRA), 0) == iota((ids.shape[0], EXTRA), 1)
    marked_ref[:, :width] = dy_ref[...]
    part = marked_ref.shape[0]
    here = (iota((part, tok), 0) + pl.program_id(0) * part == iota((part, tok), 1)).astype(BF16)
    by_token = dot_tn(ids.astype(F32).astype(BF16), own.astype(BF16)).astype(BF16)
    marked_ref[:, width:] = dot(here, by_token).astype(BF16)


def node_rows(ids_t, x, dy, nodes, local):
    top, tok = ids_t.shape
    width = x.shape[1]
    share = tok * NODES_MAX // nodes
    steps = 2
    part = tok // steps
    return pl.pallas_call(
        functools.partial(node_kernel, share=share, nodes=nodes, local=local),
        grid=(steps,),
        in_specs=[
            pl.BlockSpec((top, tok), lambda i: (0, 0)),
            pl.BlockSpec((tok, width), lambda i: (0, 0)),
            pl.BlockSpec((part, width), lambda i: (i, 0)),
        ],
        out_specs=[
            pl.BlockSpec((nodes * share // steps, width + EXTRA), lambda i: (i, 0)),
            pl.BlockSpec((part, width + EXTRA), lambda i: (i, 0)),
        ],
        out_shape=[
            jax.ShapeDtypeStruct((nodes * share, width + EXTRA), BF16),
            jax.ShapeDtypeStruct((tok, width + EXTRA), BF16),
        ],
        compiler_params=pltpu.CompilerParams(vmem_limit_bytes=VMEM),
        cost_estimate=pl.CostEstimate(
            flops=2 * nodes * share * 256 * width, bytes_accessed=7_000_000, transcendentals=0
        ),
        name="node_rows",
    )(ids_t, x, dy)


def part_kernel(me_ref, rows_ref, slots_ref, *refs, share, nodes, local):
    outs, (main_ref, tail_ref) = refs[:local], refs[local:]
    x, c = me_ref[0] // 2, me_ref[0] % 2
    half = nodes // 2
    rows = half * share
    mains = half * MAIN
    tails = 2 * nodes

    def to_of(rel):
        return ((x + rel // 2) % (local // 2)) * 2 + (c + rel) % 2

    @pl.when(pl.program_id(0) == 0)
    def _():
        col, lane = iota((local * mains, EXTRA), 0), iota((local * mains, EXTRA), 1)
        spread = (lane == to_of(col // mains)).astype(BF16)
        shape = (local * mains, rows)
        row, at = iota(shape, 0), iota(shape, 1)
        fits = at // share == (row % mains) // MAIN
        slot = (row % MAIN).astype(F32)
        for g in range(2):
            place = dot_nt(spread, slots_ref[g * rows : (g + 1) * rows, :])
            main_ref[g] = jnp.logical_and(place == slot, fits).astype(BF16)
        col, lane = iota((local * tails, EXTRA), 0), iota((local * tails, EXTRA), 1)
        spread = (lane == to_of(col // tails)).astype(BF16)
        shape = (local * tails, 2 * rows)
        row, at = iota(shape, 0), iota(shape, 1)
        place = dot_nt(spread, slots_ref[...])
        fits = at // share == (row % tails) // 2
        tail_ref[...] = jnp.logical_and(place == (MAIN + row % 2).astype(F32), fits).astype(BF16)

    for g in range(2):
        got = dot(main_ref[g], rows_ref[g * rows : (g + 1) * rows, :]).astype(BF16)
        for rel in range(local):
            outs[rel][g * mains : (g + 1) * mains, :] = got[rel * mains : (rel + 1) * mains, :]
    got = dot(tail_ref[...], rows_ref[...]).astype(BF16)
    for rel in range(local):
        outs[rel][2 * mains :, :] = got[rel * tails : (rel + 1) * tails, :]


def part_rows(me, rows, nodes, local):
    total, wide = rows.shape
    width = wide - EXTRA
    share = total // nodes
    steps = 2
    fold = width // steps
    size = nodes * CAP
    return pl.pallas_call(
        functools.partial(part_kernel, share=share, nodes=nodes, local=local),
        grid=(steps,),
        in_specs=[
            pl.BlockSpec(memory_space=pltpu.SMEM),
            pl.BlockSpec((total, fold), lambda i: (0, i)),
            pl.BlockSpec((total, EXTRA), lambda i: (0, width // EXTRA)),
        ],
        out_specs=[pl.BlockSpec((size, fold), lambda i: (0, i)) for _ in range(local)],
        out_shape=[jax.ShapeDtypeStruct((size, width), BF16) for _ in range(local)],
        scratch_shapes=[
            pltpu.VMEM((2, local * nodes // 2 * MAIN, total // 2), BF16),
            pltpu.VMEM((local * nodes * 2, total), BF16),
        ],
        compiler_params=pltpu.CompilerParams(vmem_limit_bytes=VMEM),
        cost_estimate=pl.CostEstimate(
            flops=4 * local * size * 256 * width, bytes_accessed=13_000_000, transcendentals=0
        ),
        name="part_rows",
    )(me, rows, rows)


def gathered_kernel(me_ref, *refs, tok, nodes, local):
    rows_refs, ids_refs, (out_ref, main_ref, tail_ref) = refs[:local], refs[local : 2 * local], refs[2 * local :]
    pair = 2 * MAIN
    per_node = local * CAP

    @pl.when(pl.program_id(0) == 0)
    def _():
        lane = iota((tok, EXTRA), 1)
        earlier = (iota((tok, tok), 1) < iota((tok, tok), 0)).astype(BF16)

        def place_of(ids_ref):
            ids = ids_ref[...].astype(F32)
            hit = jnp.zeros((tok, EXTRA), F32)
            for slot in range(TOP):
                hit = hit + (ids[:, slot : slot + 1] == (lane * local + me_ref[0]).astype(F32)).astype(F32)
            return jnp.where(hit > 0.5, dot(earlier, hit.astype(BF16)), -1.0).astype(BF16)

        shape = (nodes * pair, EXTRA)
        spread = (iota(shape, 0) // pair == iota(shape, 1)).astype(BF16)
        shape = (nodes * pair, 2 * tok)
        row, at = iota(shape, 0), iota(shape, 1)
        core = at // tok
        main_fits = core == (row % pair) // MAIN
        main_slot = (row % MAIN).astype(F32)
        tail_fits = core == (row % pair) // 2 % 2
        tail_slot = (MAIN + row % 2).astype(F32)
        for d in range(local // 2):
            place = jnp.concatenate([place_of(ids_refs[2 * d]), place_of(ids_refs[2 * d + 1])], axis=0)
            place = dot_nt(spread, place)
            main_ref[d] = jnp.logical_and(place == main_slot, main_fits).astype(BF16)
            here = jnp.logical_and(tail_fits, (row % pair) // 4 == d)
            tail_ref[d] = jnp.logical_and(place == tail_slot, here).astype(BF16)

    tail = None
    for d in range(local // 2):
        rows = jnp.concatenate([rows_refs[2 * d][...], rows_refs[2 * d + 1][...]], axis=0)
        got = dot(main_ref[d], rows).astype(BF16)
        for n in range(nodes):
            out_ref[n * per_node + d * pair : n * per_node + (d + 1) * pair, :] = got[n * pair : (n + 1) * pair, :]
        part = dot(tail_ref[d], rows)
        tail = part if tail is None else tail + part
    tail = tail.astype(BF16)
    for n in range(nodes):
        out_ref[n * per_node + local * MAIN : (n + 1) * per_node, :] = tail[n * pair : (n + 1) * pair, :]


def gathered_rows(me, parts, nodes, local):
    tok, wide = parts[0].shape
    width = wide - EXTRA
    tile = width // 2
    size = nodes * local * CAP
    picks = pltpu.VMEM((local // 2, nodes * 2 * MAIN, 2 * tok), BF16)
    return pl.pallas_call(
        functools.partial(gathered_kernel, tok=tok, nodes=nodes, local=local),
        grid=(width // tile,),
        in_specs=[pl.BlockSpec(memory_space=pltpu.SMEM)]
        + [pl.BlockSpec((tok, tile), lambda i: (0, i))] * local
        + [pl.BlockSpec((tok, EXTRA), lambda i: (0, width // EXTRA))] * local,
        out_specs=pl.BlockSpec((size, tile), lambda i: (0, i)),
        out_shape=jax.ShapeDtypeStruct((size, width), BF16),
        scratch_shapes=[picks, picks],
        compiler_params=pltpu.CompilerParams(vmem_limit_bytes=VMEM),
        cost_estimate=pl.CostEstimate(
            flops=4 * size * 256 * width, bytes_accessed=17_000_000, transcendentals=0
        ),
        name="gathered_rows",
    )(me, *parts, *parts)


def pre_kernel(*refs, nodes):
    rows_refs, (w_ref, out_ref, rows_ref, made_ref, sems) = refs[:-5], refs[-5:]
    count = len(rows_refs)
    size = nodes * CAP
    per_node = count * CAP

    @pl.when(pl.program_id(0) == 0)
    def _():
        copies = [
            pltpu.make_async_copy(rows_refs[i], rows_ref.at[pl.ds(i * size, size), :], sems.at[i])
            for i in range(count)
        ]
        for copy in copies:
            copy.start()
        for copy in copies:
            copy.wait()

    made_ref[...] = dot(rows_ref[...], w_ref[...])
    for n in range(nodes):
        for i in range(count):
            to, at = n * per_node + i * MAIN, i * size + n * MAIN
            out_ref[to : to + MAIN, :] = made_ref[at : at + MAIN, :]
            to, at = n * per_node + count * MAIN + i * 2, i * size + nodes * MAIN + n * 2
            out_ref[to : to + 2, :] = made_ref[at : at + 2, :]


def pre_of(parts, w_up, nodes, tile=256):
    width, hid = w_up.shape
    count = len(parts)
    total = nodes * count * CAP
    return pl.pallas_call(
        functools.partial(pre_kernel, nodes=nodes),
        grid=(hid // tile,),
        in_specs=[pl.BlockSpec(memory_space=pl.ANY)] * count + [pl.BlockSpec((width, tile), lambda i: (0, i))],
        out_specs=pl.BlockSpec((total, tile), lambda i: (0, i)),
        out_shape=jax.ShapeDtypeStruct((total, hid), F32),
        scratch_shapes=[
            pltpu.VMEM((total, width), BF16),
            pltpu.VMEM((total, tile), F32),
            pltpu.SemaphoreType.DMA((count,)),
        ],
        compiler_params=pltpu.CompilerParams(vmem_limit_bytes=VMEM),
        cost_estimate=pl.CostEstimate(
            flops=2 * total * width * hid, bytes_accessed=15_000_000, transcendentals=0
        ),
        name="pre",
    )(*parts, w_up)


def back_kernel(
    me_ref, rows_ref, early_ref, late_ref, down_ref, up_ref, out_ref, raw_ref, inner_ref, gate_ref, piece_ref, stack_ref, fold_ref, extra_ref, sems, pre_ref, *, local
):
    step = pl.program_id(0)
    width = down_ref.shape[1]
    tile = down_ref.shape[0]
    hid = inner_ref.shape[1]
    main = out_ref.shape[0]
    fold = width // QUARTERS
    tails = 2 * GROUP
    size = GROUP * MAIN
    groups = main // size
    first = hid // tile

    for j in range(first):

        @pl.when(step == j)
        def _():
            mains, lasts = local // 2 * MAIN, local // 2 * 2
            half = mains + lasts
            for n in range(main // (local * MAIN)):
                for h, ref in enumerate((early_ref, late_ref)):
                    to = n * 2 * half + h * mains
                    pre_ref[to : to + mains, :] = ref[n * half : n * half + mains, :]
                    to = n * 2 * half + 2 * mains + h * lasts
                    pre_ref[to : to + lasts, :] = ref[n * half + mains : (n + 1) * half, :]
            pre = pre_ref[...]
            back = dot_nt(rows_ref[...], down_ref[...])
            sig = 1.0 / (1.0 + jnp.exp(-pre))
            act = (pre * sig).astype(BF16).astype(F32)
            raw_ref[:, j * tile : (j + 1) * tile] = (back * sig * (1.0 + pre * (1.0 - sig))).astype(BF16)
            gate = jnp.sum(act * back, axis=-1, keepdims=True)
            gate_ref[...] = gate if j == 0 else gate_ref[...] + gate

    def return_order():
        x, c = me_ref[0] // 2, me_ref[0] % 2
        rows = size + tails
        to, at = iota((rows, rows), 0), iota((rows, rows), 1)
        is_main = to < size
        source = jnp.where(is_main, to // MAIN, (to - size) // 2)
        node, place = source // local, source % local
        rel = ((x + local // 2 - place // 2) % (local // 2)) * 2 + (place + c) % 2
        start = jnp.where(is_main, rel * MAIN + to % MAIN, local * MAIN + rel * 2 + to % 2)
        return (at == node * (local * CAP) + start).astype(BF16)

    def copy_of(q):
        return pltpu.make_async_copy(
            piece_ref.at[q % 2], out_ref.at[:, pl.ds(q * fold, fold)], sems.at[q % 2]
        )

    fold_copy = pltpu.make_async_copy(fold_ref, out_ref.at[:, pl.ds(width, fold)], sems.at[2])
    extra_copy = pltpu.make_async_copy(extra_ref, out_ref.at[:, pl.ds(width + fold, EXTRA)], sems.at[3])

    for q in range(QUARTERS):

        @pl.when(step == first + q)
        def _():
            if q == 0:
                order = return_order()
                rows = size + tails
                for b in range(groups):
                    got = dot(order, raw_ref[b * rows : (b + 1) * rows, :]).astype(BF16)
                    inner_ref[b * size : (b + 1) * size, :] = got[:size, :]
                    inner_ref[main + b * tails : main + (b + 1) * tails, :] = got[size:, :]
            if q >= 2:
                copy_of(q - 2).wait()
            piece_ref[q % 2] = dot_nt(inner_ref[:main, :], up_ref[...]).astype(BF16)
            copy_of(q).start()
            if q == 0:
                pick = (iota((size, tails), 0) // MAIN == iota((size, tails), 1) // 2).astype(BF16)
                parity = iota((size, EXTRA), 0) % 2
                low = iota((size, EXTRA), 1) < EXTRA // 2
                for b in range(groups):
                    gates = jnp.broadcast_to(gate_ref[b * rows : (b + 1) * rows, :], (rows, EXTRA))
                    gates = dot(order, gates.astype(BF16))
                    mains, last = gates[:size, :], gates[size:, :]
                    odd = (iota((tails, EXTRA), 0) % 2 == 1)
                    even_rows = dot(pick, jnp.where(odd, 0.0, last).astype(BF16))
                    odd_rows = dot(pick, jnp.where(odd, last, 0.0).astype(BF16))
                    tail_rows = jnp.where(parity == 1, odd_rows, even_rows)
                    extra_ref[b * size : (b + 1) * size, :] = jnp.where(
                        low, mains, tail_rows
                    ).astype(BF16)
                extra_copy.start()
            piece = dot_nt(inner_ref[main:, :], up_ref[...]).astype(BF16)
            for b in range(groups):
                stack_ref[b * size + q * tails : b * size + (q + 1) * tails, :] = piece[b * tails : (b + 1) * tails, :]
            if q == QUARTERS - 1:
                to = iota((size, size), 0)
                source = ((to % MAIN) // 2) * tails + (to // MAIN) * 2 + to % 2
                order = (source == iota((size, size), 1)).astype(BF16)
                for b in range(groups):
                    fold_ref[b * size : (b + 1) * size, :] = dot(
                        order, stack_ref[b * size : (b + 1) * size, :]
                    ).astype(BF16)
                fold_copy.start()
                copy_of(q - 1).wait()
                copy_of(q).wait()
                extra_copy.wait()
                fold_copy.wait()


def pieces_of(me, rows, early, late, w_down, w_up, local, tile=256):
    total, width = rows.shape
    hid = w_down.shape[0]
    main = total // CAP * MAIN
    fold = width // QUARTERS
    first = hid // tile
    return pl.pallas_call(
        functools.partial(back_kernel, local=local),
        grid=(first + QUARTERS,),
        in_specs=[
            pl.BlockSpec(memory_space=pltpu.SMEM),
            pl.BlockSpec((total, width), lambda i: (0, 0), pipeline_mode=pl.Buffered(1)),
            pl.BlockSpec((total // 2, tile), lambda i: (0, jnp.minimum(i, first - 1))),
            pl.BlockSpec((total // 2, tile), lambda i: (0, jnp.minimum(i, first - 1))),
            pl.BlockSpec((tile, width), lambda i: (jnp.minimum(i, first - 1), 0)),
            pl.BlockSpec((fold, hid), lambda i: (jnp.maximum(i - first, 0), 0)),
        ],
        out_specs=pl.BlockSpec(memory_space=pl.ANY),
        out_shape=jax.ShapeDtypeStruct((main, width + fold + EXTRA), BF16),
        scratch_shapes=[
            pltpu.VMEM((total, hid), BF16),
            pltpu.VMEM((total, hid), BF16),
            pltpu.VMEM((total, 1), F32),
            pltpu.VMEM((2, main, fold), BF16),
            pltpu.VMEM((main, fold), BF16),
            pltpu.VMEM((main, fold), BF16),
            pltpu.VMEM((main, EXTRA), BF16),
            pltpu.SemaphoreType.DMA((4,)),
            pltpu.VMEM((total, tile), F32),
        ],
        compiler_params=pltpu.CompilerParams(vmem_limit_bytes=VMEM),
        cost_estimate=pl.CostEstimate(
            flops=4 * total * width * hid, bytes_accessed=39_000_000, transcendentals=total * hid
        ),
        name="back_and_pieces",
    )(me, rows, early, late, w_down, w_up)


def combine_kernel(ids_ref, gate_ref, rows_ref, fold_ref, extra_ref, out_ref, grad_ref, main_ref, last_ref, tail_ref):
    step = pl.program_id(0)
    top, tok = ids_ref.shape
    fold = fold_ref.shape[1]
    size = GROUP * MAIN
    tails = 2 * GROUP
    groups = rows_ref.shape[0] // size

    @pl.when(step == 0)
    def _():
        ids = ids_ref[...]
        to = iota((size, size), 0)
        unfold = ((to % tails) // 2) * MAIN + (to // tails) * 2 + to % 2
        unfold = (unfold == iota((size, size), 1)).astype(BF16)
        spread = (iota((size, GROUP), 0) // MAIN == iota((size, GROUP), 1)).astype(BF16)
        twice = (iota((tails, GROUP), 0) // 2 == iota((tails, GROUP), 1)).astype(BF16)
        row, last_row = iota((size, tok), 0), iota((tails, tok), 0)
        grads = [jnp.zeros((1, tok), F32) for _ in range(top)]
        for b in range(groups):
            place, expert = places(ids, b * GROUP, GROUP)
            place = place.astype(BF16)
            high = jnp.zeros(expert.shape, F32)
            low = jnp.zeros(expert.shape, F32)
            for slot in range(top):
                same = expert == ids[slot : slot + 1, :]
                fixed = gate_ref[slot : slot + 1, :]
                high = high + jnp.where(same, (fixed // 256).astype(F32), 0.0)
                low = low + jnp.where(same, (fixed % 256).astype(F32), 0.0)
            gates = jnp.concatenate([high, low], axis=1).astype(BF16)

            def weights(copies, slots):
                mask = dot(copies, place) == slots.astype(F32)
                both = dot(copies, gates)
                scaled = [both[:, :tok] * (1.0 / 256.0), both[:, tok:] * (1.0 / 65536.0)]
                return mask, jnp.concatenate([jnp.where(mask, part, 0.0) for part in scaled], axis=1)

            main, weight = weights(spread, row % MAIN)
            main_ref[:, b * size : (b + 1) * size] = weight.T.astype(BF16)
            tail, weight = weights(twice, MAIN + last_row % 2)
            last_ref[:, b * tails : (b + 1) * tails] = weight.T.astype(BF16)
            stack = dot(unfold, fold_ref[b * size : (b + 1) * size, :]).astype(BF16)
            for q in range(QUARTERS):
                tail_ref[q, b * tails : (b + 1) * tails, :] = stack[q * tails : (q + 1) * tails, :]
            extra = extra_ref[b * size : (b + 1) * size, :]
            value = jnp.where(main, extra[:, 0:1].astype(F32), 0.0)
            last = dot(unfold[:tails, :], extra)[:, EXTRA // 2 : EXTRA // 2 + 1]
            last = jnp.where(tail, last, 0.0)
            value = dot_tn(spread, value.astype(BF16)) + dot_tn(twice, last.astype(BF16))
            for slot in range(top):
                same = expert == ids[slot : slot + 1, :]
                grads[slot] = grads[slot] + jnp.sum(jnp.where(same, value, 0.0), axis=0, keepdims=True)
        grad_ref[...] = jnp.concatenate(grads, axis=0).astype(BF16)

    both = dot(main_ref[...], rows_ref[...]) + dot(last_ref[...], tail_ref[step])
    out_ref[...] = (both[:tok, :] + both[tok:, :]).astype(BF16)


def combine(ids_t, gate_t, rows, width):
    top, tok = ids_t.shape
    main, wide = rows.shape
    fold = width // QUARTERS
    tails = main // QUARTERS
    return pl.pallas_call(
        combine_kernel,
        grid=(QUARTERS,),
        in_specs=[
            pl.BlockSpec((top, tok), lambda i: (0, 0)),
            pl.BlockSpec((top, tok), lambda i: (0, 0)),
            pl.BlockSpec((main, fold), lambda i: (0, i)),
            pl.BlockSpec((main, fold), lambda i: (0, QUARTERS)),
            pl.BlockSpec((main, EXTRA), lambda i: (0, (width + fold) // EXTRA)),
        ],
        out_specs=[
            pl.BlockSpec((tok, fold), lambda i: (0, i)),
            pl.BlockSpec((top, tok), lambda i: (0, 0)),
        ],
        out_shape=[
            jax.ShapeDtypeStruct((tok, width), BF16),
            jax.ShapeDtypeStruct((top, tok), BF16),
        ],
        scratch_shapes=[
            pltpu.VMEM((2 * tok, main), BF16),
            pltpu.VMEM((2 * tok, tails), BF16),
            pltpu.VMEM((QUARTERS, tails, fold), BF16),
        ],
        compiler_params=pltpu.CompilerParams(vmem_limit_bytes=VMEM),
        name="combine",
    )(ids_t, gate_t, rows, rows, rows)


def exchange(rows, axes):
    count = lax.axis_size(axes)
    blocks = rows.reshape(count, rows.shape[0] // count, rows.shape[1])
    blocks = lax.all_to_all(blocks, axes, split_axis=0, concat_axis=0, tiled=True)
    return blocks.reshape(rows.shape)


def shift(rows, rel, local):
    chips = local // 2
    pairs = [(2 * x + c, 2 * ((x + rel // 2) % chips) + (c + rel) % 2) for x in range(chips) for c in range(2)]
    return lax.ppermute(rows, "local", pairs)


def per_device(tokens, cotangent, expert_ids, gate_fixed, w_up, w_down):
    nodes, local = lax.axis_size("node"), lax.axis_size("local")
    width = tokens.shape[1]
    ids_t = expert_ids.T
    gate_t = gate_fixed.T
    me = lax.axis_index("local").astype(jnp.int32).reshape(1)
    send_x, marked = node_rows(ids_t, tokens, cotangent, nodes, local)
    rows_x = exchange(send_x, "node")
    same = [marked] + [shift(marked, 2 * d, local) for d in range(1, local // 2)]
    all_dy = [part for rows in same for part in (rows, shift(rows, 1, local))]
    rows_dy = exchange(gathered_rows(me, all_dy, nodes, local), "node")
    parts = part_rows(me, rows_x, nodes, local)
    parts = [parts[0]] + [shift(parts[rel], rel, local) for rel in range(1, local)]
    early = pre_of(parts[: local // 2], w_up[0], nodes)
    late = pre_of(parts[local // 2 :], w_up[0], nodes)
    pieces = pieces_of(me, rows_dy, early, late, w_down[0], w_up[0], local)
    grad_input, grad_gate = combine(ids_t, gate_t, exchange(pieces, ("node", "local")), width)
    return grad_input, grad_gate.T


def solution(mesh):
    split = P(("node", "local"), None)
    experts = P(("node", "local"), None, None)
    return jax.shard_map(
        per_device,
        mesh=mesh,
        in_specs=(split, split, split, split, experts, experts),
        out_specs=(split, split),
        check_vma=False,
    )
```
